32 devices in a mesh: shard: 4 (over x, core), ctx: 2 (over y), tp: 4 (over z).
Axes of the slice: x: 2, y: 2, z: 4, core: 2. Of those that a mesh axis runs over, the one named last changes fastest.
Arguments:
- tokens: bfloat16 [4096, 960], P(('shard', 'ctx', 'tp')), may hold values from -6 to 6
- positions: int32 [4096], P('shard'), may hold values from 0 to 1023, as said below
- norm1_gain: bfloat16 [960], P('shard'), may hold values from 0.25 to 1.75
- w_query: bfloat16 [960, 960], P('shard'), may hold values from -0.1875 to 0.1875
- w_key: bfloat16 [960, 320], P('shard'), may hold values from -0.1875 to 0.1875
- w_value: bfloat16 [960, 320], P('shard'), may hold values from -0.1875 to 0.1875
- w_out: bfloat16 [960, 960], P('shard'), may hold values from -6 to 6
- norm2_gain: bfloat16 [960], P('shard'), may hold values from 0.25 to 1.75
- w_gate: bfloat16 [960, 2560], P('shard', 'tp'), may hold values from -0.1875 to 0.1875
- w_up: bfloat16 [960, 2560], P('shard', 'tp'), may hold values from -0.1875 to 0.1875
- w_down: bfloat16 [2560, 960], P('tp', 'shard'), may hold values from -0.125 to 0.125
- out_grad: bfloat16 [4096, 960], P(('shard', 'ctx', 'tp')), may hold values from -6 to 6
Outputs:
- result: bfloat16 [4096, 960], P(('shard', 'ctx', 'tp'))
- tokens_grad: bfloat16 [4096, 960], P(('shard', 'ctx', 'tp'))
- norm1_gain_grad: float32 [960], P('shard')
- w_query_grad: float32 [960, 960], P('shard')
- w_key_grad: float32 [960, 320], P('shard')
- w_value_grad: float32 [960, 320], P('shard')
- w_out_grad: float32 [960, 960], P('shard')
- norm2_gain_grad: float32 [960], P('shard')
- w_gate_grad: float32 [960, 2560], P('shard', 'tp')
- w_up_grad: float32 [960, 2560], P('shard', 'tp')
- w_down_grad: float32 [2560, 960], P('tp', 'shard')
The draws below stay inside these ranges and needn't reach their ends.
Inputs may be any that keep to these rules, and one draw needn't show every extreme that they name: `positions`: in each sequence every place 0 to 1023 appears once. The sequence consists of 4 blocks of 256 places; its rows run over the ctx ranks, within a rank over the tp ranks, then over two halves of 64 rows each. Rank c holds in its first half block b_c and in its second half block 3 - b_c, where b is a permutation of 0 to 1 drawn for each sequence; tp rank t holds places t * 64 to t * 64 + 63 of each of these blocks, in order.
All inputs are finite; a program needn't handle non-finite values.
Results may differ from the reference program's by a relative error of at most 0.025.
Values may be sent and summed in bfloat16 or wider, within the bound.
A program may use at most 128 MiB of HBM per device.

```python
import math
import jax
import jax.numpy as jnp
from jax import lax

D = 960
QUERY_HEADS = 15
KEY_VALUE_HEADS = 5
HEAD_SIZE = 64
FF = 2560
QB = 64
SEQUENCE_TOKENS = 1024
TOKENS = 4096
KV = 320
N_SHARD = 4
N_CTX = 2
N_TP = 4


def draw_positions(key, part):
    block_width = QB * N_TP
    seq_keys = jax.random.split(key, N_SHARD)
    pair_order = jax.vmap(lambda single: jax.random.permutation(single, N_CTX))(seq_keys).astype(jnp.int32)
    early_block = pair_order[:, :, None, None, None]
    late_block = 2 * N_CTX - 1 - early_block
    which_half = jnp.arange(2, dtype=jnp.int32)[None, None, None, :, None]
    chosen = jnp.where(which_half == 0, early_block, late_block)
    tp_rank = jnp.arange(N_TP, dtype=jnp.int32)[None, None, :, None, None]
    row_index = jnp.arange(QB, dtype=jnp.int32)[None, None, None, None, :]
    placed = chosen * block_width + tp_rank * QB + row_index
    return placed.reshape(N_SHARD * N_CTX * N_TP * 2 * QB).astype(jnp.int32)


def block_levels(stream_key, shape, pieces, low, high):
    def one(axis_at, shards_of):
        steps = jax.random.uniform(jax.random.fold_in(jax.random.fold_in(stream_key, 6), axis_at), (shards_of,), jnp.float32, low / len(pieces), high / len(pieces))
        return jnp.repeat(jnp.exp(steps), shape[axis_at] // shards_of).reshape((-1,) + (1,) * (len(shape) - axis_at - 1))

    gain = one(*pieces[0])
    for cut in pieces[1:]:
        gain = gain * one(*cut)
    return gain


def gaussian(stream_key, shape, scale, bound, pieces=(), kind=jnp.bfloat16):
    gain = block_levels(stream_key, shape, pieces, -0.22, 0.18) if pieces else 1.0
    drawn = jax.random.normal(stream_key, shape, jnp.float32) * scale * gain
    return jnp.minimum(jnp.maximum(drawn, -bound), bound).astype(kind)


def setup_inputs(seed: int = 0) -> dict:
    splits = jax.random.split(jax.random.key(seed), 13)
    tokens = gaussian(splits[0], (TOKENS, D), 1.0, 6.0, ((0, 32),))
    positions = draw_positions(jax.random.fold_in(splits[12], 71), 0)
    norm1_gain = jnp.clip(1.0 + 0.15 * jax.random.normal(splits[2], (D,), jnp.float32), 0.25, 1.75).astype(jnp.bfloat16)
    w_query = gaussian(splits[3], (D, D), D ** -0.5, 0.1875, ((0, 4),))
    w_key = gaussian(splits[4], (D, KV), D ** -0.5, 0.1875, ((0, 4),))
    w_value = gaussian(splits[5], (D, KV), D ** -0.5, 0.1875, ((0, 4),))
    w_out = gaussian(splits[6], (D, D), 1 ** -0.5, 6.0, ((0, 4),))
    norm2_gain = jnp.clip(1.0 + 0.15 * jax.random.normal(splits[7], (D,), jnp.float32), 0.25, 1.75).astype(jnp.bfloat16)
    w_gate = gaussian(splits[8], (D, FF), D ** -0.5, 0.1875, ((0, 4), (1, 4)))
    w_up = gaussian(splits[9], (D, FF), D ** -0.5, 0.1875, ((0, 4), (1, 4)))
    w_down = gaussian(splits[10], (FF, D), FF ** -0.5, 0.125, ((0, 4), (1, 4)))
    out_grad = gaussian(splits[11], (TOKENS, D), 1.0, 6.0, ((0, 32),))
    return dict(tokens=tokens, positions=positions, norm1_gain=norm1_gain, w_query=w_query, w_key=w_key, w_value=w_value, w_out=w_out, norm2_gain=norm2_gain, w_gate=w_gate, w_up=w_up, w_down=w_down, out_grad=out_grad)


norm_eps = 1e-05
rope_base = 100000.0
negative_large = -1e+30

@jax.custom_vjp
def lower_half(v):
    return lax.optimization_barrier(v.astype(jnp.bfloat16)).astype(jnp.float32)

@jax.custom_vjp
def lower_backward(v):
    return v

def low_keep(v):
    return (lower_half(v), None)

def low_pass(kept, grad):
    return (grad,)

def back_keep(v):
    return (v, None)

def back_low(kept, grad):
    return (lower_half(grad),)
lower_half.defvjp(low_keep, low_pass)
lower_backward.defvjp(back_keep, back_low)

def rope_tables(block_places, head_width):
    half_width = head_width // 2
    frequency = rope_base ** (-(jnp.arange(half_width, dtype=jnp.float32) * 2.0 / head_width))
    angles = block_places.astype(jnp.float32)[:, None] * frequency[None, :]
    return (jnp.cos(angles), jnp.sin(angles))

def apply_rotary(heads, cosine_table, sine_table):
    half_width = heads.shape[-1] // 2
    first = heads[..., :half_width]
    second = heads[..., half_width:]
    cosine_rows = cosine_table[:, None, :]
    sine_rows = sine_table[:, None, :]
    return jnp.concatenate([first * cosine_rows - second * sine_rows, second * cosine_rows + first * sine_rows], axis=-1)

def layer(rows, block_places, gain_one, query_w, key_w, value_weight, out_w, gain_two, gate_w, up_w, down_w):
    highest_precision = lax.Precision.HIGHEST
    query_groups = QUERY_HEADS // KEY_VALUE_HEADS
    head_scale = 1.0 / math.sqrt(HEAD_SIZE)
    normed_one = rows * lax.rsqrt(lax.optimization_barrier(jnp.mean(rows * rows, axis=-1, keepdims=True)) + norm_eps)
    first_hidden = lower_half(normed_one * gain_one)
    unrotated_query = lower_backward(jnp.dot(first_hidden, query_w, precision=highest_precision))
    unrotated_key = lower_backward(jnp.dot(first_hidden, key_w, precision=highest_precision))
    value_tensor = lower_half(lower_backward(jnp.dot(first_hidden, value_weight, precision=highest_precision))).reshape(SEQUENCE_TOKENS, KEY_VALUE_HEADS, HEAD_SIZE)
    cosine_table, sine_table = rope_tables(block_places, HEAD_SIZE)
    query_tensor = lower_half(apply_rotary(unrotated_query.reshape(SEQUENCE_TOKENS, QUERY_HEADS, HEAD_SIZE), cosine_table, sine_table)).reshape(SEQUENCE_TOKENS, KEY_VALUE_HEADS, query_groups, HEAD_SIZE)
    key_tensor = lower_half(apply_rotary(unrotated_key.reshape(SEQUENCE_TOKENS, KEY_VALUE_HEADS, HEAD_SIZE), cosine_table, sine_table))
    block_size = 512 if SEQUENCE_TOKENS % 512 == 0 else SEQUENCE_TOKENS
    pair_count = SEQUENCE_TOKENS // block_size

    def attend_blocks(items):
        query_block, place_block = items
        scores = jnp.einsum('qhgd,khd->hgqk', query_block, key_tensor, precision=highest_precision)
        scores = lower_backward(scores * head_scale)
        allowed = block_places[None, :] <= place_block[:, None]
        scores = jnp.where(allowed, scores, negative_large)
        weights = jax.nn.softmax(scores, axis=-1)
        return jnp.einsum('hgqk,khd->qhgd', lower_half(weights), value_tensor, precision=highest_precision)
    attention_output = lax.map(jax.checkpoint(attend_blocks), (query_tensor.reshape(pair_count, block_size, KEY_VALUE_HEADS, query_groups, HEAD_SIZE), block_places.reshape(pair_count, block_size)))
    attention_output = lower_half(lower_backward(attention_output.reshape(SEQUENCE_TOKENS, QUERY_HEADS * HEAD_SIZE)))
    middle = rows + lower_backward(jnp.dot(attention_output, out_w, precision=highest_precision))
    normed_two = middle * lax.rsqrt(lax.optimization_barrier(jnp.mean(middle * middle, axis=-1, keepdims=True)) + norm_eps)
    hidden_two = lower_half(normed_two * gain_two)
    gate = lower_backward(jnp.dot(hidden_two, gate_w, precision=highest_precision))
    upper = lower_backward(jnp.dot(hidden_two, up_w, precision=highest_precision))
    inner = lower_half(gate * jax.nn.sigmoid(gate) * upper)
    return middle + jnp.dot(inner, down_w, precision=highest_precision)

def reference(tokens, positions, norm1_gain, w_query, w_key, w_value, w_out, norm2_gain, w_gate, w_up, w_down, out_grad):
    params = (norm1_gain.astype(jnp.float32), w_query.astype(jnp.float32), w_key.astype(jnp.float32), w_value.astype(jnp.float32), w_out.astype(jnp.float32), norm2_gain.astype(jnp.float32), w_gate.astype(jnp.float32), w_up.astype(jnp.float32), w_down.astype(jnp.float32))
    seq_rows = tokens.astype(jnp.float32).reshape(N_SHARD, SEQUENCE_TOKENS, D)
    seq_places = positions.reshape(N_SHARD, SEQUENCE_TOKENS).astype(jnp.int32)
    seq_cotangent = out_grad.astype(jnp.float32).reshape(N_SHARD, SEQUENCE_TOKENS, D)
    start_totals = tuple((jnp.zeros(weight.shape, jnp.float32) for weight in params))

    def one_sequence(totals, items):
        rows, block_places, cotangent = items

        def forward(inputs, *weights):
            return layer(inputs, block_places, *weights)
        output, pullback = jax.vjp(forward, rows, *params)
        grads = pullback(cotangent)
        totals = tuple((total + piece for total, piece in zip(totals, grads[1:])))
        return (totals, (output.astype(jnp.bfloat16), grads[0].astype(jnp.bfloat16)))
    totals, (outputs, input_grads) = lax.scan(one_sequence, start_totals, (seq_rows, seq_places, seq_cotangent))
    return (outputs.reshape(TOKENS, D), input_grads.reshape(TOKENS, D), totals[0], totals[1], totals[2], totals[3], totals[4], totals[5], totals[6], totals[7], totals[8])
```

```python
import functools
import math

import jax
import jax.numpy as jnp
from jax import lax
from jax.experimental import pallas as pl
from jax.experimental.pallas import tpu as pltpu
from jax.sharding import PartitionSpec as P

QUERY_HEADS = 15
KEY_VALUE_HEADS = 5
HEAD_SIZE = 64


norm_eps = 1e-05
rope_base = 100000.0
negative_large = -1e30


def rope_tables(block_places, head_width):
    half_width = head_width // 2
    frequency = rope_base ** (-(jnp.arange(half_width, dtype=jnp.float32) * 2.0 / head_width))
    angles = block_places.astype(jnp.float32)[:, None] * frequency[None, :]
    return (jnp.cos(angles), jnp.sin(angles))


def apply_rotary(heads, cosine_table, sine_table):
    half_width = heads.shape[-1] // 2
    first = heads[..., :half_width]
    second = heads[..., half_width:]
    cosine_rows = cosine_table[:, None, :]
    sine_rows = sine_table[:, None, :]
    return jnp.concatenate(
        [first * cosine_rows - second * sine_rows, second * cosine_rows + first * sine_rows],
        axis=-1,
    )


def norm_rows(rows):
    inverse = lax.rsqrt(jnp.mean(rows * rows, axis=-1, keepdims=True) + norm_eps)
    return (rows * inverse, inverse)


def norm_back(grad_normed, normed, inverse, gain):
    scaled = grad_normed * gain
    grad_rows = inverse * (scaled - normed * jnp.mean(scaled * normed, axis=-1, keepdims=True))
    return (grad_rows, jnp.sum(grad_normed * normed, axis=0))


MESH = pl.DeviceIdType.MESH
HBM = pl.BlockSpec(memory_space=pl.ANY)


def group_size(kind):
    shard, ctx, tp = lax.axis_size("shard"), lax.axis_size("ctx"), lax.axis_size("tp")
    return {"core": 2, "x": shard // 2, "shard": shard, "ctx": ctx, "tp": tp, "all": ctx * tp}[kind]


def group_place(kind):
    shard, ctx, tp = lax.axis_index("shard"), lax.axis_index("ctx"), lax.axis_index("tp")
    if kind == "core":
        return lax.rem(shard, 2)
    if kind == "x":
        return lax.div(shard, 2)
    if kind == "all":
        return ctx * lax.axis_size("tp") + tp
    return {"shard": shard, "ctx": ctx, "tp": tp}[kind]


def member(kind, step):
    size = group_size(kind)
    place = lax.rem(group_place(kind) + step, size)
    if kind == "core":
        return place, {"shard": 2 * lax.div(lax.axis_index("shard"), 2) + place}
    if kind == "x":
        return place, {"shard": 2 * place + lax.rem(lax.axis_index("shard"), 2)}
    if kind == "all":
        tp = lax.axis_size("tp")
        return place, {"ctx": lax.div(place, tp), "tp": lax.rem(place, tp)}
    return place, {kind: place}


def greet(kinds):
    barrier = pltpu.get_barrier_semaphore()
    total = 0
    for kind in kinds:
        for step in range(1, group_size(kind)):
            _, device = member(kind, step)
            pl.semaphore_signal(barrier, inc=1, device_id=device, device_id_type=MESH)
            total += 1
    pl.semaphore_wait(barrier, total)


def send(src, dst, sems, index, device):
    copy = pltpu.make_async_remote_copy(
        src_ref=src,
        dst_ref=dst,
        send_sem=sems.at[0, index],
        recv_sem=sems.at[1, index],
        device_id=device,
        device_id_type=MESH,
    )
    copy.start()
    return copy


def exchange_body(plan, *refs):
    count = len(plan)
    ins, outs, sems, local = refs[:count], refs[count : 2 * count], refs[-2], refs[-1]
    greet(sorted({kind for kind, _ in plan}))
    copies = []
    own = []
    index = 0
    for item, (kind, mode) in enumerate(plan):
        me = group_place(kind)
        if mode == "gather":
            copy = pltpu.make_async_copy(ins[item], outs[item].at[me], local.at[item])
            copy.start()
            own.append(copy)
    for item, (kind, mode) in enumerate(plan):
        me = group_place(kind)
        for step in range(1, group_size(kind)):
            place, device = member(kind, step)
            if mode == "gather":
                source, target = ins[item], outs[item].at[me]
            elif mode == "second":
                source, target = ins[item].at[:, place], outs[item].at[step - 1]
            else:
                source, target = ins[item].at[place], outs[item].at[step - 1]
            copies.append(send(source, target, sems, index, device))
            index += 1
    for copy in own:
        copy.wait()
    for copy in copies:
        copy.wait()


def exchange(collective_id, *items):
    plan = tuple((kind, mode) for _, kind, mode in items)
    shapes = []
    total = 0
    for array, kind, mode in items:
        size = group_size(kind)
        total += size - 1
        if mode == "gather":
            shape = (size,) + array.shape
        elif mode == "second":
            shape = (size - 1,) + array.shape[:1] + array.shape[2:]
        else:
            shape = (size - 1,) + array.shape[1:]
        shapes.append(jax.ShapeDtypeStruct(shape, array.dtype))
    return pl.pallas_call(
        functools.partial(exchange_body, plan),
        out_shape=shapes,
        in_specs=[HBM] * len(items),
        out_specs=[HBM] * len(items),
        scratch_shapes=[
            pltpu.SemaphoreType.DMA((2, total)),
            pltpu.SemaphoreType.DMA((len(items),)),
        ],
        compiler_params=pltpu.CompilerParams(collective_id=collective_id, has_side_effects=True),
    )(*[array for array, _, _ in items])


def spread_body(count, *refs):
    ins, outs, sems, local = refs[:count], refs[count : 2 * count], refs[-2], refs[-1]
    greet(("ctx", "tp"))
    ctx, tp = group_place("ctx"), group_place("tp")
    size_ctx, size_tp = group_size("ctx"), group_size("tp")
    own = []
    across = []
    onward = []
    index = 0
    for item in range(count):
        copy = pltpu.make_async_copy(ins[item], outs[item].at[ctx, tp], local.at[item])
        copy.start()
        own.append(copy)
        for step in range(1, size_tp):
            _, device = member("tp", step)
            target = outs[item].at[ctx, tp]
            across.append((item, step, send(ins[item], target, sems, index, device)))
            index += 1
        for hop in range(1, size_ctx):
            _, device = member("ctx", hop)
            target = outs[item].at[ctx, tp]
            onward.append(send(ins[item], target, sems, index, device))
            index += 1
    for item, step, copy in across:
        copy.wait_recv()
        source = outs[item].at[ctx, lax.rem(tp + size_tp - step, size_tp)]
        for hop in range(1, size_ctx):
            _, device = member("ctx", hop)
            onward.append(send(source, source, sems, index, device))
            index += 1
    for _, _, copy in across:
        copy.wait_send()
    for copy in onward:
        copy.wait()
    for copy in own:
        copy.wait()


def spread(collective_id, *arrays):
    size_ctx, size_tp = group_size("ctx"), group_size("tp")
    total = len(arrays) * (size_ctx * size_tp - 1)
    return pl.pallas_call(
        functools.partial(spread_body, len(arrays)),
        out_shape=[
            jax.ShapeDtypeStruct((size_ctx, size_tp) + array.shape, array.dtype)
            for array in arrays
        ],
        in_specs=[HBM] * len(arrays),
        out_specs=[HBM] * len(arrays),
        scratch_shapes=[
            pltpu.SemaphoreType.DMA((2, total)),
            pltpu.SemaphoreType.DMA((len(arrays),)),
        ],
        compiler_params=pltpu.CompilerParams(collective_id=collective_id, has_side_effects=True),
    )(*arrays)


def pair_device():
    ctx = lax.axis_index("ctx")
    return {"ctx": 2 * lax.div(ctx, 2) + 1 - lax.rem(ctx, 2)}


def weights_body(halves, *refs):
    count = len(halves)
    ins, outs = refs[: count + 2], refs[count + 2 : 2 * count + 4]
    sems, local = refs[-2], refs[-1]
    shard, parity = group_place("shard"), lax.rem(lax.axis_index("ctx"), 2)
    size_x = group_size("x")
    sibling = member("core", 1)[1]
    partner = pair_device()
    barrier = pltpu.get_barrier_semaphore()
    peers = [sibling, partner]
    peers += [member("x", step)[1] for step in range(1, size_x)]
    peers += [member("shard", step)[1] for step in range(1, group_size("shard"))]
    peers += [member("tp", step)[1] for step in range(1, group_size("tp"))]
    for device in peers:
        pl.semaphore_signal(barrier, inc=1, device_id=device, device_id_type=MESH)
    pl.semaphore_wait(barrier, len(peers))

    def remote(src, dst, index, device):
        return pltpu.make_async_remote_copy(
            src_ref=src,
            dst_ref=dst,
            send_sem=sems.at[0, index],
            recv_sem=sems.at[1, index],
            device_id=device,
            device_id_type=MESH,
        )

    plain = []
    for item in range(count + 2):
        place = shard if item <= count else group_place("tp")
        copy = pltpu.make_async_copy(ins[item], outs[item].at[place], local.at[item])
        copy.start()
        plain.append(copy)
    index = 0
    across = {}
    for item in range(count):
        for step in range(1, size_x):
            _, device = member("x", step)
            copy = remote(ins[item], outs[item].at[shard], index, device)
            across[item, step] = copy
            index += 1

            @pl.when(parity == halves[item])
            def _():
                copy.start()

    for step in range(1, group_size("shard")):
        _, device = member("shard", step)
        plain.append(send(ins[count], outs[count].at[shard], sems, index, device))
        index += 1
    for step in range(1, group_size("tp")):
        _, device = member("tp", step)
        target = outs[count + 1].at[group_place("tp")]
        plain.append(send(ins[count + 1], target, sems, index, device))
        index += 1
    for item in range(count):
        plain.append(send(ins[item], outs[item].at[shard], sems, index, sibling))
        index += 1
    handed = {}
    for step in range(1, size_x):
        origin = lax.rem(shard + 2 * (size_x - step), 2 * size_x)
        for item in range(count):
            block = outs[item].at[origin]
            handed[item, step] = (
                remote(block, block, index, partner),
                remote(block, block, index + 1, sibling),
            )
            index += 2
    for parity_now in range(2):

        @pl.when(parity == parity_now)
        def _():
            mine = [key for key in handed if halves[key[0]] == parity_now]
            others = [key for key in handed if halves[key[0]] != parity_now]
            for one, two in zip(mine, others):
                across[one].wait_recv()
                handed[one][0].start()
                handed[one][1].start()
                handed[two][0].wait_recv()
                handed[two][1].start()
            for key in mine[len(others) :]:
                across[key].wait_recv()
                handed[key][0].start()
                handed[key][1].start()
            for key in others[len(mine) :]:
                handed[key][0].wait_recv()
                handed[key][1].start()
            for key in mine:
                across[key].wait_send()
                handed[key][0].wait_send()

    for key in handed:
        handed[key][1].wait()
    for copy in plain:
        copy.wait()


def gather_weights(collective_id, halves, weights, gains, rows):
    shard, tp = group_size("shard"), group_size("tp")
    count = len(weights)
    total = count * (shard // 2 - 1) * 3 + count + shard - 1 + tp - 1
    return pl.pallas_call(
        functools.partial(weights_body, halves),
        out_shape=[
            jax.ShapeDtypeStruct((shard,) + array.shape, array.dtype)
            for array in (*weights, gains)
        ]
        + [jax.ShapeDtypeStruct((tp,) + rows.shape, rows.dtype)],
        in_specs=[HBM] * (count + 2),
        out_specs=[HBM] * (count + 2),
        scratch_shapes=[
            pltpu.SemaphoreType.DMA((2, total)),
            pltpu.SemaphoreType.DMA((count + 2,)),
        ],
        compiler_params=pltpu.CompilerParams(collective_id=collective_id, has_side_effects=True),
    )(*weights, gains, rows)


def total_of(own, others):
    return own.astype(jnp.float32) + jnp.sum(others.astype(jnp.float32), axis=0)


def own_block(array, kind, axis=0):
    return lax.dynamic_index_in_dim(array, group_place(kind), axis, keepdims=False)


def per_device(
    tokens,
    positions,
    norm1_gain,
    w_query,
    w_key,
    w_value,
    w_out,
    norm2_gain,
    w_gate,
    w_up,
    w_down,
    out_grad,
):
    piece = norm1_gain.shape[0]
    gains = jnp.stack([norm1_gain, norm2_gain])
    gains = jnp.pad(gains, ((0, 14), (0, -piece % 128)))
    qkv_w, gate_w, out_w, up_w, down_w, gains, grad_all = gather_weights(
        1,
        (0, 0, 1, 1, 1),
        (jnp.concatenate([w_query, w_key, w_value], axis=1), w_gate, w_out, w_up, w_down.T),
        gains,
        out_grad,
    )
    qkv_w, gate_w, out_w, up_w, down_w, grad_all = (
        array.reshape(-1, array.shape[-1])
        for array in (qkv_w, gate_w, out_w, up_w, down_w, grad_all)
    )
    gain_one = gains[:, 0, :piece].reshape(-1)
    gain_two = gains[:, 1, :piece].reshape(-1)
    shard_rows = tokens.shape[0]
    width = tokens.shape[1]
    seq_len = positions.shape[0]
    query_groups = QUERY_HEADS // KEY_VALUE_HEADS
    key_value_width = KEY_VALUE_HEADS * HEAD_SIZE
    head_scale = 1.0 / math.sqrt(HEAD_SIZE)
    gain_one = gain_one.astype(jnp.float32)
    gain_two = gain_two.astype(jnp.float32)
    group_rank = lax.axis_index("ctx") * lax.axis_size("tp") + lax.axis_index("tp")
    own_place = lax.dynamic_slice_in_dim(positions, group_rank * shard_rows, shard_rows)
    residual = tokens.astype(jnp.float32)
    normed_one, inverse_one = norm_rows(residual)
    first_hidden = (normed_one * gain_one).astype(jnp.bfloat16)
    projected = jnp.dot(first_hidden, qkv_w, preferred_element_type=jnp.float32)
    unrotated_query = projected[:, :width]
    unrotated_key = projected[:, width : width + key_value_width]
    value_rows = projected[:, width + key_value_width :].astype(jnp.bfloat16)
    cosine_table, sine_table = rope_tables(own_place, HEAD_SIZE)
    query_tensor = apply_rotary(
        unrotated_query.reshape(shard_rows, QUERY_HEADS, HEAD_SIZE), cosine_table, sine_table
    ).astype(jnp.bfloat16)
    query_tensor = query_tensor.reshape(shard_rows, KEY_VALUE_HEADS, query_groups, HEAD_SIZE)
    key_row_list = apply_rotary(
        unrotated_key.reshape(shard_rows, KEY_VALUE_HEADS, HEAD_SIZE), cosine_table, sine_table
    ).astype(jnp.bfloat16)
    key_row_list = key_row_list.reshape(shard_rows, key_value_width)
    (gathered,) = spread(2, jnp.concatenate([key_row_list, value_rows], axis=1))
    gathered = gathered.reshape(seq_len, 2 * key_value_width)
    gathered_keys = gathered[:, :key_value_width]
    gathered_values = gathered[:, key_value_width:]
    block_size = 512
    pair_count = seq_len // block_size
    blocked_keys = gathered_keys.reshape(pair_count, block_size, KEY_VALUE_HEADS, HEAD_SIZE)
    blocked_values = gathered_values.reshape(pair_count, block_size, KEY_VALUE_HEADS, HEAD_SIZE)
    place_blocks = positions.reshape(pair_count, block_size)

    def forward_block(carry, items):
        run_max, run_total, run_acc = carry
        key_block, value_block, key_place = items
        allowed = key_place[None, :] <= own_place[:, None]
        scores = (
            jnp.einsum(
                "qhgd,khd->hgqk", query_tensor, key_block, preferred_element_type=jnp.float32
            )
            * head_scale
        )
        scores = jnp.where(allowed, scores, negative_large)
        new_max = jnp.maximum(run_max, jnp.max(scores, axis=-1))
        weights = jnp.where(allowed, jnp.exp(scores - new_max[..., None]), 0.0)
        factor = jnp.exp(run_max - new_max)
        run_total = run_total * factor + jnp.sum(weights, axis=-1)
        run_acc = run_acc * factor[..., None] + jnp.einsum(
            "hgqk,khd->hgqd",
            weights.astype(jnp.bfloat16),
            value_block,
            preferred_element_type=jnp.float32,
        )
        return ((new_max, run_total, run_acc), None)

    start_carry = (
        jnp.full((KEY_VALUE_HEADS, query_groups, shard_rows), negative_large, jnp.float32),
        jnp.zeros((KEY_VALUE_HEADS, query_groups, shard_rows), jnp.float32),
        jnp.zeros((KEY_VALUE_HEADS, query_groups, shard_rows, HEAD_SIZE), jnp.float32),
    )
    (run_max, run_total, run_acc), _ = lax.scan(
        forward_block, start_carry, (blocked_keys, blocked_values, place_blocks)
    )
    log_total = run_max + jnp.log(run_total)
    attention_output = jnp.transpose(run_acc / run_total[..., None], (2, 0, 1, 3))
    attention_low = attention_output.reshape(shard_rows, width).astype(jnp.bfloat16)
    middle = residual + jnp.dot(attention_low, out_w, preferred_element_type=jnp.float32)
    normed_two, inverse_two = norm_rows(middle)
    hidden_two = (normed_two * gain_two).astype(jnp.bfloat16)
    (mlp_input,) = exchange(3, (hidden_two, "tp", "gather"))
    mlp_input = mlp_input.reshape(-1, width)
    gate = jnp.dot(mlp_input, gate_w, preferred_element_type=jnp.float32)
    upper = jnp.dot(mlp_input, up_w, preferred_element_type=jnp.float32)
    sigma = jax.nn.sigmoid(gate)
    active = gate * sigma
    inner = (active * upper).astype(jnp.bfloat16)
    mlp_output = jnp.einsum("rf,df->rd", inner, down_w, preferred_element_type=jnp.float32)
    mlp_output = mlp_output.astype(jnp.bfloat16).reshape(-1, shard_rows, width)
    grad_inner = jnp.einsum("rd,df->rf", grad_all, down_w, preferred_element_type=jnp.float32)
    grad_down_w = jnp.einsum("rf,rd->df", inner, grad_all, preferred_element_type=jnp.float32)
    grad_gate = (grad_inner * upper * sigma * (1.0 + gate * (1.0 - sigma))).astype(jnp.bfloat16)
    grad_upper = (grad_inner * active).astype(jnp.bfloat16)
    grad_gate_w = jnp.einsum("rd,rf->df", mlp_input, grad_gate, preferred_element_type=jnp.float32)
    grad_up_w = jnp.einsum("rd,rf->df", mlp_input, grad_upper, preferred_element_type=jnp.float32)
    grad_hidden_two = (
        jnp.einsum("rf,df->rd", grad_gate, gate_w, preferred_element_type=jnp.float32)
        + jnp.einsum("rf,df->rd", grad_upper, up_w, preferred_element_type=jnp.float32)
    ).astype(jnp.bfloat16)
    grad_hidden_two = grad_hidden_two.reshape(-1, shard_rows, width)
    hidden_terms, output_terms = exchange(
        4, (grad_hidden_two, "tp", "first"), (mlp_output, "tp", "first")
    )
    grad_hidden_two = total_of(own_block(grad_hidden_two, "tp"), hidden_terms)
    result = (middle + total_of(own_block(mlp_output, "tp"), output_terms)).astype(jnp.bfloat16)
    grad_middle_norm, grad_gain_two = norm_back(grad_hidden_two, normed_two, inverse_two, gain_two)
    grad_middle = out_grad.astype(jnp.float32) + grad_middle_norm
    grad_middle_low = grad_middle.astype(jnp.bfloat16)
    grad_out_w = jnp.einsum(
        "rc,rd->cd", attention_low, grad_middle_low, preferred_element_type=jnp.float32
    )
    attention_gradient = jnp.einsum(
        "rd,cd->rc", grad_middle_low, out_w, preferred_element_type=jnp.float32
    )
    attention_gradient = attention_gradient.astype(jnp.bfloat16).reshape(
        shard_rows, KEY_VALUE_HEADS, query_groups, HEAD_SIZE
    )
    delta = jnp.einsum("qhgd,qhgd->hgq", attention_gradient.astype(jnp.float32), attention_output)

    def score_grads(key_block, value_block, key_place):
        allowed = key_place[None, :] <= own_place[:, None]
        scores = (
            jnp.einsum(
                "qhgd,khd->hgqk", query_tensor, key_block, preferred_element_type=jnp.float32
            )
            * head_scale
        )
        scores = jnp.where(allowed, scores, negative_large)
        weights = jnp.where(allowed, jnp.exp(scores - log_total[..., None]), 0.0)
        grad_weights = jnp.einsum(
            "qhgd,khd->hgqk", attention_gradient, value_block, preferred_element_type=jnp.float32
        )
        grad_scores = (weights * (grad_weights - delta[..., None])).astype(jnp.bfloat16)
        return (weights.astype(jnp.bfloat16), grad_scores)

    def key_value_terms(weights_low, grad_scores):
        grad_key = (
            jnp.einsum(
                "hgqk,qhgd->khd", grad_scores, query_tensor, preferred_element_type=jnp.float32
            )
            * head_scale
        )
        grad_value = jnp.einsum(
            "hgqk,qhgd->khd", weights_low, attention_gradient, preferred_element_type=jnp.float32
        )
        return (grad_key, grad_value)

    def query_term(grad_scores, key_block):
        return (
            jnp.einsum("hgqk,khd->qhgd", grad_scores, key_block, preferred_element_type=jnp.float32)
            * head_scale
        )

    query_offset = jnp.zeros((shard_rows, KEY_VALUE_HEADS, query_groups, HEAD_SIZE), jnp.float32)

    def backward_block(grad_query, items):
        key_block, value_block, key_place = items
        weights_low, grad_scores = score_grads(key_block, value_block, key_place)
        grad_key, grad_value = key_value_terms(weights_low, grad_scores)
        return (grad_query + query_term(grad_scores, key_block), (grad_key, grad_value))

    grad_query, (key_terms, value_terms) = lax.scan(
        backward_block, query_offset, (blocked_keys, blocked_values, place_blocks)
    )
    pair_terms = jnp.concatenate(
        [
            key_terms.reshape(-1, shard_rows, key_value_width),
            value_terms.reshape(-1, shard_rows, key_value_width),
        ],
        axis=-1,
    ).astype(jnp.bfloat16)
    (other_terms,) = exchange(5, (pair_terms, "all", "first"))
    pair_grads = total_of(own_block(pair_terms, "all"), other_terms)
    local_key_gradient = pair_grads[:, :key_value_width]
    grad_value_own = pair_grads[:, key_value_width:]
    grad_query_raw = (
        apply_rotary(
            grad_query.reshape(shard_rows, QUERY_HEADS, HEAD_SIZE), cosine_table, -sine_table
        )
        .astype(jnp.bfloat16)
        .reshape(shard_rows, width)
    )
    grad_key_raw = (
        apply_rotary(
            local_key_gradient.reshape(shard_rows, KEY_VALUE_HEADS, HEAD_SIZE),
            cosine_table,
            -sine_table,
        )
        .astype(jnp.bfloat16)
        .reshape(shard_rows, key_value_width)
    )
    grad_value_low = grad_value_own.astype(jnp.bfloat16)
    grad_projected = jnp.concatenate([grad_query_raw, grad_key_raw, grad_value_low], axis=1)
    grad_qkv_w = jnp.einsum(
        "rd,rc->dc", first_hidden, grad_projected, preferred_element_type=jnp.float32
    )
    grad_hidden_one = jnp.einsum(
        "rc,dc->rd", grad_projected, qkv_w, preferred_element_type=jnp.float32
    )
    grad_residual_norm, grad_gain_one = norm_back(
        grad_hidden_one, normed_one, inverse_one, gain_one
    )
    tokens_grad = (grad_middle + grad_residual_norm).astype(jnp.bfloat16)
    size_shard, size_x, size_ctx = group_size("shard"), group_size("x"), group_size("ctx")
    size_tp = group_size("tp")
    gain_grads = jnp.stack([grad_gain_one, grad_gain_two]).reshape(2, size_shard, piece)
    gain_grads = jnp.pad(gain_grads.transpose(1, 0, 2), ((0, 0), (0, 6), (0, -piece % 128)))
    partial = [
        array.astype(jnp.bfloat16).reshape(size_x, 2, piece, array.shape[-1])
        for array in (grad_qkv_w, grad_gate_w, grad_out_w, grad_up_w, grad_down_w)
    ]
    *others, other_gains = exchange(
        6, *[(array, "core", "second") for array in partial], (gain_grads, "shard", "first")
    )
    gain_grads = total_of(own_block(gain_grads, "shard"), other_gains)
    cut = [
        total_of(own_block(array, "core", 1), other)
        .astype(jnp.bfloat16)
        .reshape(size_x, piece, size_ctx, array.shape[-1] // size_ctx)
        for array, other in zip(partial, others)
    ]
    early = jnp.concatenate(cut[:2], axis=-1).transpose(0, 2, 1, 3)
    late = jnp.concatenate(cut[2:], axis=-1).transpose(2, 0, 1, 3)
    early_others, late_others, gain_all = exchange(
        7, (early, "x", "first"), (late, "ctx", "first"), (gain_grads, "all", "gather")
    )
    early = total_of(own_block(early, "x"), early_others).astype(jnp.bfloat16)
    late = total_of(own_block(late, "ctx"), late_others).astype(jnp.bfloat16)
    early_others, late_others = exchange(8, (early, "ctx", "first"), (late, "x", "first"))
    early = total_of(own_block(early, "ctx"), early_others)
    late = total_of(own_block(late, "x"), late_others)
    qkv_part = qkv_w.shape[-1] // size_ctx
    out_part = width // size_ctx
    feed = jnp.concatenate([early[:, qkv_part:], late[:, out_part:]], axis=1).astype(jnp.bfloat16)
    attend = jnp.concatenate([early[:, :qkv_part], late[:, :out_part]], axis=1)
    attend = attend.astype(jnp.bfloat16).reshape(piece, size_tp, -1).transpose(1, 0, 2)
    attend_others, feed = exchange(9, (attend, "tp", "first"), (feed, "ctx", "gather"))
    attend = total_of(own_block(attend, "tp"), attend_others).astype(jnp.bfloat16)
    (attend,) = spread(10, attend)
    attend = attend.transpose(2, 0, 1, 3).reshape(piece, size_ctx, -1).astype(jnp.float32)
    feed = feed.transpose(1, 0, 2).astype(jnp.float32)
    out_qkv = attend[:, :, :qkv_part].reshape(piece, -1)
    out_query = out_qkv[:, :width]
    out_key = out_qkv[:, width : width + key_value_width]
    out_value = out_qkv[:, width + key_value_width :]
    out_proj = attend[:, :, qkv_part:].reshape(piece, -1)
    hidden_part = gate_w.shape[-1] // size_ctx
    out_gate = feed[:, :, :hidden_part].reshape(piece, -1)
    out_up = feed[:, :, hidden_part : 2 * hidden_part].reshape(piece, -1)
    out_down = feed[:, :, 2 * hidden_part :].reshape(piece, -1).T
    gain_total = jnp.sum(gain_all, axis=0)
    out_gain_one = gain_total[0, :piece]
    out_gain_two = gain_total[1, :piece]
    return (
        result,
        tokens_grad,
        out_gain_one,
        out_query,
        out_key,
        out_value,
        out_proj,
        out_gain_two,
        out_gate,
        out_up,
        out_down,
    )


def solution(mesh):
    in_specs = (
        P(("shard", "ctx", "tp"), None),
        P("shard"),
        P("shard"),
        P("shard", None),
        P("shard", None),
        P("shard", None),
        P("shard", None),
        P("shard"),
        P("shard", "tp"),
        P("shard", "tp"),
        P("tp", "shard"),
        P(("shard", "ctx", "tp"), None),
    )
    out_specs = (
        P(("shard", "ctx", "tp"), None),
        P(("shard", "ctx", "tp"), None),
        P("shard"),
        P("shard", None),
        P("shard", None),
        P("shard", None),
        P("shard", None),
        P("shard"),
        P("shard", "tp"),
        P("shard", "tp"),
        P("tp", "shard"),
    )
    return jax.shard_map(
        per_device, mesh=mesh, in_specs=in_specs, out_specs=out_specs, check_vma=False
    )
```

```python
import functools
import math

import jax
import jax.numpy as jnp
from jax import lax
from jax.experimental import pallas as pl
from jax.experimental.pallas import tpu as pltpu
from jax.sharding import PartitionSpec as P

QUERY_HEADS = 15
KEY_VALUE_HEADS = 5
HEAD_SIZE = 64


norm_eps = 1e-05
rope_base = 100000.0
negative_large = -1e30


def rope_tables(block_places, head_width):
    half_width = head_width // 2
    frequency = rope_base ** (-(jnp.arange(half_width, dtype=jnp.float32) * 2.0 / head_width))
    angles = block_places.astype(jnp.float32)[:, None] * frequency[None, :]
    return (jnp.cos(angles), jnp.sin(angles))


def apply_rotary(heads, cosine_table, sine_table):
    half_width = heads.shape[-1] // 2
    first = heads[..., :half_width]
    second = heads[..., half_width:]
    cosine_rows = cosine_table[:, None, :]
    sine_rows = sine_table[:, None, :]
    return jnp.concatenate(
        [first * cosine_rows - second * sine_rows, second * cosine_rows + first * sine_rows],
        axis=-1,
    )


def norm_rows(rows):
    inverse = lax.rsqrt(jnp.mean(rows * rows, axis=-1, keepdims=True) + norm_eps)
    return (rows * inverse, inverse)


def norm_back(grad_normed, normed, inverse, gain):
    scaled = grad_normed * gain
    grad_rows = inverse * (scaled - normed * jnp.mean(scaled * normed, axis=-1, keepdims=True))
    return (grad_rows, jnp.sum(grad_normed * normed, axis=0))


MESH = pl.DeviceIdType.MESH
HBM = pl.BlockSpec(memory_space=pl.ANY)


def group_size(kind):
    shard, ctx, tp = lax.axis_size("shard"), lax.axis_size("ctx"), lax.axis_size("tp")
    return {"core": 2, "x": shard // 2, "shard": shard, "ctx": ctx, "tp": tp, "all": ctx * tp}[kind]


def group_place(kind):
    shard, ctx, tp = lax.axis_index("shard"), lax.axis_index("ctx"), lax.axis_index("tp")
    if kind == "core":
        return lax.rem(shard, 2)
    if kind == "x":
        return lax.div(shard, 2)
    if kind == "all":
        return ctx * lax.axis_size("tp") + tp
    return {"shard": shard, "ctx": ctx, "tp": tp}[kind]


def member(kind, step):
    size = group_size(kind)
    place = lax.rem(group_place(kind) + step, size)
    if kind == "core":
        return place, {"shard": 2 * lax.div(lax.axis_index("shard"), 2) + place}
    if kind == "x":
        return place, {"shard": 2 * place + lax.rem(lax.axis_index("shard"), 2)}
    if kind == "all":
        tp = lax.axis_size("tp")
        return place, {"ctx": lax.div(place, tp), "tp": lax.rem(place, tp)}
    return place, {kind: place}


def greet(kinds):
    barrier = pltpu.get_barrier_semaphore()
    total = 0
    for kind in kinds:
        for step in range(1, group_size(kind)):
            _, device = member(kind, step)
            pl.semaphore_signal(barrier, inc=1, device_id=device, device_id_type=MESH)
            total += 1
    pl.semaphore_wait(barrier, total)


def send(src, dst, sems, index, device):
    copy = pltpu.make_async_remote_copy(
        src_ref=src,
        dst_ref=dst,
        send_sem=sems.at[0, index],
        recv_sem=sems.at[1, index],
        device_id=device,
        device_id_type=MESH,
    )
    copy.start()
    return copy


def exchange_body(plan, *refs):
    count = len(plan)
    ins, outs, sems, local = refs[:count], refs[count : 2 * count], refs[-2], refs[-1]
    greet(sorted({kind for kind, _ in plan}))
    copies = []
    own = []
    index = 0
    for item, (kind, mode) in enumerate(plan):
        me = group_place(kind)
        if mode == "gather":
            copy = pltpu.make_async_copy(ins[item], outs[item].at[me], local.at[item])
            copy.start()
            own.append(copy)
    for item, (kind, mode) in enumerate(plan):
        me = group_place(kind)
        for step in range(1, group_size(kind)):
            place, device = member(kind, step)
            if mode == "gather":
                source, target = ins[item], outs[item].at[me]
            elif mode == "second":
                source, target = ins[item].at[:, place], outs[item].at[step - 1]
            else:
                source, target = ins[item].at[place], outs[item].at[step - 1]
            copies.append(send(source, target, sems, index, device))
            index += 1
    for copy in own:
        copy.wait()
    for copy in copies:
        copy.wait()


def exchange(collective_id, *items):
    plan = tuple((kind, mode) for _, kind, mode in items)
    shapes = []
    total = 0
    for array, kind, mode in items:
        size = group_size(kind)
        total += size - 1
        if mode == "gather":
            shape = (size,) + array.shape
        elif mode == "second":
            shape = (size - 1,) + array.shape[:1] + array.shape[2:]
        else:
            shape = (size - 1,) + array.shape[1:]
        shapes.append(jax.ShapeDtypeStruct(shape, array.dtype))
    return pl.pallas_call(
        functools.partial(exchange_body, plan),
        out_shape=shapes,
        in_specs=[HBM] * len(items),
        out_specs=[HBM] * len(items),
        scratch_shapes=[
            pltpu.SemaphoreType.DMA((2, total)),
            pltpu.SemaphoreType.DMA((len(items),)),
        ],
        compiler_params=pltpu.CompilerParams(collective_id=collective_id, has_side_effects=True),
    )(*[array for array, _, _ in items])


def spread_body(count, *refs):
    ins, outs, sems, local = refs[:count], refs[count : 2 * count], refs[-2], refs[-1]
    greet(("ctx", "tp"))
    ctx, tp = group_place("ctx"), group_place("tp")
    size_ctx, size_tp = group_size("ctx"), group_size("tp")
    own = []
    across = []
    onward = []
    index = 0
    for item in range(count):
        copy = pltpu.make_async_copy(ins[item], outs[item].at[ctx, tp], local.at[item])
        copy.start()
        own.append(copy)
        for step in range(1, size_tp):
            _, device = member("tp", step)
            target = outs[item].at[ctx, tp]
            across.append((item, step, send(ins[item], target, sems, index, device)))
            index += 1
        for hop in range(1, size_ctx):
            _, device = member("ctx", hop)
            target = outs[item].at[ctx, tp]
            onward.append(send(ins[item], target, sems, index, device))
            index += 1
    for item, step, copy in across:
        copy.wait_recv()
        source = outs[item].at[ctx, lax.rem(tp + size_tp - step, size_tp)]
        for hop in range(1, size_ctx):
            _, device = member("ctx", hop)
            onward.append(send(source, source, sems, index, device))
            index += 1
    for _, _, copy in across:
        copy.wait_send()
    for copy in onward:
        copy.wait()
    for copy in own:
        copy.wait()


def spread(collective_id, *arrays):
    size_ctx, size_tp = group_size("ctx"), group_size("tp")
    total = len(arrays) * (size_ctx * size_tp - 1)
    return pl.pallas_call(
        functools.partial(spread_body, len(arrays)),
        out_shape=[
            jax.ShapeDtypeStruct((size_ctx, size_tp) + array.shape, array.dtype)
            for array in arrays
        ],
        in_specs=[HBM] * len(arrays),
        out_specs=[HBM] * len(arrays),
        scratch_shapes=[
            pltpu.SemaphoreType.DMA((2, total)),
            pltpu.SemaphoreType.DMA((len(arrays),)),
        ],
        compiler_params=pltpu.CompilerParams(collective_id=collective_id, has_side_effects=True),
    )(*arrays)


def pair_device():
    ctx = lax.axis_index("ctx")
    return {"ctx": 2 * lax.div(ctx, 2) + 1 - lax.rem(ctx, 2)}


def weights_body(halves, *refs):
    count = len(halves)
    ins, outs = refs[: count + 2], refs[count + 2 : 2 * count + 4]
    sems, local = refs[-2], refs[-1]
    shard, parity = group_place("shard"), lax.rem(lax.axis_index("ctx"), 2)
    size_x = group_size("x")
    sibling = member("core", 1)[1]
    partner = pair_device()
    barrier = pltpu.get_barrier_semaphore()
    peers = [sibling, partner]
    peers += [member("x", step)[1] for step in range(1, size_x)]
    peers += [member("shard", step)[1] for step in range(1, group_size("shard"))]
    peers += [member("tp", step)[1] for step in range(1, group_size("tp"))]
    for device in peers:
        pl.semaphore_signal(barrier, inc=1, device_id=device, device_id_type=MESH)
    pl.semaphore_wait(barrier, len(peers))

    def remote(src, dst, index, device):
        return pltpu.make_async_remote_copy(
            src_ref=src,
            dst_ref=dst,
            send_sem=sems.at[0, index],
            recv_sem=sems.at[1, index],
            device_id=device,
            device_id_type=MESH,
        )

    plain = []
    for item in range(count + 2):
        place = shard if item <= count else group_place("tp")
        copy = pltpu.make_async_copy(ins[item], outs[item].at[place], local.at[item])
        copy.start()
        plain.append(copy)
    index = 0
    across = {}
    pieces = 3 if ins[0].shape[0] % 48 == 0 else 1
    height = ins[0].shape[0] // pieces
    for item in range(count):
        for part in range(pieces):
            cut = pl.ds(part * height, height)
            for step in range(1, size_x):
                _, device = member("x", step)
                target = outs[item].at[shard, cut]
                across[item, part, step] = remote(ins[item].at[cut], target, index, device)
                index += 1
    ahead = 3 * (size_x - 1)
    for parity_now in range(2):

        @pl.when(parity == parity_now)
        def _():
            mine = [key for key in across if halves[key[0]] == parity_now]
            for key in mine[:ahead]:
                across[key].start()

    for step in range(1, group_size("shard")):
        _, device = member("shard", step)
        plain.append(send(ins[count], outs[count].at[shard], sems, index, device))
        index += 1
    for step in range(1, group_size("tp")):
        _, device = member("tp", step)
        target = outs[count + 1].at[group_place("tp")]
        plain.append(send(ins[count + 1], target, sems, index, device))
        index += 1
    for item in range(count):
        plain.append(send(ins[item], outs[item].at[shard], sems, index, sibling))
        index += 1
    handed = {}
    for item, part, step in across:
        origin = lax.rem(shard + 2 * (size_x - step), 2 * size_x)
        block = outs[item].at[origin, pl.ds(part * height, height)]
        handed[item, part, step] = (
            remote(block, block, index, partner),
            remote(block, block, index + 1, sibling),
        )
        index += 2
    lag = 2
    for parity_now in range(2):

        @pl.when(parity == parity_now)
        def _():
            mine = [key for key in handed if halves[key[0]] == parity_now]
            others = [key for key in handed if halves[key[0]] != parity_now]
            for turn in range(max(len(mine), len(others) + lag)):
                if turn < len(mine):
                    key = mine[turn]
                    across[key].wait_recv()
                    handed[key][0].start()
                    handed[key][1].start()
                    across[key].wait_send()
                    if turn + ahead < len(mine):
                        across[mine[turn + ahead]].start()
                if lag <= turn < len(others) + lag:
                    key = others[turn - lag]
                    handed[key][0].wait_recv()
                    handed[key][1].start()
            for key in mine:
                handed[key][0].wait_send()

    for key in handed:
        handed[key][1].wait()
    for copy in plain:
        copy.wait()


def gather_weights(collective_id, halves, weights, gains, rows):
    shard, tp = group_size("shard"), group_size("tp")
    count = len(weights)
    pieces = 3 if weights[0].shape[0] % 48 == 0 else 1
    total = count * pieces * (shard // 2 - 1) * 3 + count + shard - 1 + tp - 1
    return pl.pallas_call(
        functools.partial(weights_body, halves),
        out_shape=[
            jax.ShapeDtypeStruct((shard,) + array.shape, array.dtype)
            for array in (*weights, gains)
        ]
        + [jax.ShapeDtypeStruct((tp,) + rows.shape, rows.dtype)],
        in_specs=[HBM] * (count + 2),
        out_specs=[HBM] * (count + 2),
        scratch_shapes=[
            pltpu.SemaphoreType.DMA((2, total)),
            pltpu.SemaphoreType.DMA((count + 2,)),
        ],
        compiler_params=pltpu.CompilerParams(collective_id=collective_id, has_side_effects=True),
    )(*weights, gains, rows)


def reduce_body(sizes, *refs):
    attn, gate, up, down, gains, terms, attn_out, feed_out, gain_out, terms_in = refs[:10]
    from_core, feed_core, attn_x, attn_x_in, attn_sum, attn_ctx_in, attn_part = refs[10:17]
    attn_tp_in, feed_sum, feed_ctx_in, feed_mid, feed_x_in, gain_in, gain_sum, sems = refs[17:]
    piece, padded = sizes
    size_x, size_ctx, size_tp = group_size("x"), group_size("ctx"), group_size("tp")
    size_shard, size_all = group_size("shard"), group_size("all")
    rows, columns = padded // size_ctx, attn.shape[-1] // size_tp
    feeds = (gate, up, down)
    hidden = gate.shape[-1]
    x, core, ctx, tp = (group_place(kind) for kind in ("x", "core", "ctx", "tp"))
    shard, all_place = group_place("shard"), group_place("all")
    greet(("shard", "all"))
    used = []

    def start(src, dst, device):
        copy = send(src, dst, sems, len(used), device)
        used.append(copy)
        return copy

    def arrived(copies):
        for copy in copies:
            copy.wait_recv()

    def add(target, *terms):
        total = terms[0].astype(jnp.float32)
        for term in terms[1:]:
            total = total + term.astype(jnp.float32)
        return total.astype(target.dtype)

    other, sibling = member("core", 1)
    attn_core = [
        start(attn.at[2 * block + other], from_core.at[block], sibling) for block in range(size_x)
    ]
    feed_core_copies = [
        start(
            feeds[item].at[2 * block + other],
            feed_core.at[item, block],
            sibling,
        )
        for item in range(3)
        for block in range(size_x)
    ]
    gain_copies = []
    for step in range(1, size_shard):
        place, device = member("shard", step)
        gain_copies.append(start(gains.at[place], gain_in.at[step - 1], device))
    term_copies = []
    for step in range(1, size_tp):
        place, device = member("tp", step)
        term_copies.append(start(terms.at[place], terms_in.at[step - 1], device))

    if padded > piece:
        attn_x[:, piece:, :] = jnp.zeros((size_x, padded - piece, attn.shape[-1]), attn.dtype)
        feed_sum[:, piece:, :] = jnp.zeros((size_x, padded - piece, 3 * hidden), attn.dtype)
    arrived(attn_core)
    for block in range(size_x):
        for at in range(0, attn.shape[-1], 640):
            cut = slice(at, at + 640)
            attn_x[block, :piece, cut] = add(
                attn_x, attn[2 * block + core, :, cut], from_core[block, :, cut]
            )
    attn_x_copies = []
    for step in range(1, size_x):
        place, device = member("x", step)
        attn_x_copies.append(start(attn_x.at[place], attn_x_in.at[step - 1], device))

    arrived(feed_core_copies)
    for item in range(3):
        for block in range(size_x):
            cut = slice(item * hidden, (item + 1) * hidden)
            feed_sum[block, :piece, cut] = add(
                feed_sum, feeds[item][2 * block + core], feed_core[item, block]
            )
    feed_ctx_copies = []
    for step in range(1, size_ctx):
        place, device = member("ctx", step)
        first = pl.multiple_of(place * rows, rows)
        feed_ctx_copies.append(
            start(feed_sum.at[:, pl.ds(first, rows)], feed_ctx_in.at[step - 1], device)
        )
    my_rows = pl.ds(pl.multiple_of(ctx * rows, rows), rows)

    arrived(gain_copies)
    gain_sum[...] = gains[shard] + jnp.sum(gain_in[...], axis=0)
    gain_out[all_place] = gain_sum[...]
    gain_last = []
    for step in range(1, size_all):
        _, device = member("all", step)
        gain_last.append(start(gain_sum, gain_out.at[all_place], device))

    arrived(feed_ctx_copies)
    for at in range(0, 3 * hidden, 640):
        cut = slice(at, at + 640)
        for block in range(size_x):
            feed_mid[block, :, cut] = add(
                feed_mid,
                feed_sum[block, my_rows, cut],
                *[feed_ctx_in[step, block, :, cut] for step in range(size_ctx - 1)],
            )
    feed_x_copies = []
    for step in range(1, size_x):
        place, device = member("x", step)
        feed_x_copies.append(start(feed_mid.at[place], feed_x_in.at[step - 1], device))

    arrived(attn_x_copies)
    for at in range(0, attn.shape[-1], 640):
        cut = slice(at, at + 640)
        attn_sum[:, cut] = add(
            attn_sum, attn_x[x, :, cut], *[attn_x_in[step, :, cut] for step in range(size_x - 1)]
        )
    attn_ctx_copies = []
    for step in range(1, size_ctx):
        place, device = member("ctx", step)
        first = pl.multiple_of(place * rows, rows)
        attn_ctx_copies.append(
            start(attn_sum.at[pl.ds(first, rows)], attn_ctx_in.at[step - 1], device)
        )

    arrived(attn_ctx_copies)
    for part in range(size_tp):
        cut = slice(part * columns, (part + 1) * columns)
        attn_part[part] = add(
            attn_part,
            attn_sum[my_rows, cut],
            *[attn_ctx_in[step, :, cut] for step in range(size_ctx - 1)],
        )
    attn_tp_copies = []
    for step in range(1, size_tp):
        place, device = member("tp", step)
        attn_tp_copies.append(start(attn_part.at[place], attn_tp_in.at[step - 1], device))

    arrived(feed_x_copies)
    for at in range(0, 3 * hidden, 640):
        cut = slice(at, at + 640)
        feed_out[ctx, :, cut] = add(
            feed_out, feed_mid[x, :, cut], *[feed_x_in[step, :, cut] for step in range(size_x - 1)]
        )
    feed_last = []
    for step in range(1, size_ctx):
        _, device = member("ctx", step)
        feed_last.append(start(feed_out.at[ctx], feed_out.at[ctx], device))

    arrived(attn_tp_copies)
    attn_out[ctx, tp] = add(
        attn_out, attn_part[tp], *[attn_tp_in[step] for step in range(size_tp - 1)]
    )
    mine = attn_out.at[ctx, tp]
    across = []
    last = []
    for step in range(1, size_tp):
        _, device = member("tp", step)
        across.append((step, start(mine, mine, device)))
    for hop in range(1, size_ctx):
        _, device = member("ctx", hop)
        last.append(start(mine, mine, device))
    for step, copy in across:
        copy.wait_recv()
        block = attn_out.at[ctx, lax.rem(tp + size_tp - step, size_tp)]
        for hop in range(1, size_ctx):
            _, device = member("ctx", hop)
            last.append(start(block, block, device))
    arrived(last)
    arrived(feed_last)
    arrived(gain_last)
    arrived(term_copies)
    for copy in used:
        copy.wait_send()


def reduce_weights(collective_id, attn, gate, up, down, gains, terms):
    size_shard, size_x, size_ctx = group_size("shard"), group_size("x"), group_size("ctx")
    size_tp, size_all = group_size("tp"), group_size("all")
    piece, width, hidden = attn.shape[1], attn.shape[2], gate.shape[2]
    unit = 16 * size_ctx
    padded = -(-piece // unit) * unit
    rows, columns = padded // size_ctx, width // size_tp
    low = attn.dtype
    total = 4 * size_x + size_shard - 1 + 2 * (size_x - 1) + 3 * (size_ctx - 1)
    total += 2 * (size_all - 1) + 2 * (size_tp - 1)
    vmem = pl.BlockSpec(memory_space=pltpu.VMEM)
    return pl.pallas_call(
        functools.partial(reduce_body, (piece, padded)),
        out_shape=[
            jax.ShapeDtypeStruct((size_ctx, size_tp, rows, columns), low),
            jax.ShapeDtypeStruct((size_ctx, rows, 3 * hidden), low),
            jax.ShapeDtypeStruct((size_all,) + gains.shape[1:], gains.dtype),
            jax.ShapeDtypeStruct((size_tp - 1,) + terms.shape[1:], terms.dtype),
        ],
        in_specs=[vmem] * 5 + [HBM],
        out_specs=[vmem] * 3 + [HBM],
        scratch_shapes=[
            pltpu.VMEM((size_x, piece, width), low),
            pltpu.VMEM((3, size_x, piece, hidden), low),
            pltpu.VMEM((size_x, padded, width), low),
            pltpu.VMEM((size_x - 1, padded, width), low),
            pltpu.VMEM((padded, width), low),
            pltpu.VMEM((size_ctx - 1, rows, width), low),
            pltpu.VMEM((size_tp, rows, columns), low),
            pltpu.VMEM((size_tp - 1, rows, columns), low),
            pltpu.VMEM((size_x, padded, 3 * hidden), low),
            pltpu.VMEM((size_ctx - 1, size_x, rows, 3 * hidden), low),
            pltpu.VMEM((size_x, rows, 3 * hidden), low),
            pltpu.VMEM((size_x - 1, rows, 3 * hidden), low),
            pltpu.VMEM((size_shard - 1,) + gains.shape[1:], gains.dtype),
            pltpu.VMEM(gains.shape[1:], gains.dtype),
            pltpu.SemaphoreType.DMA((2, total)),
        ],
        compiler_params=pltpu.CompilerParams(
            collective_id=collective_id, has_side_effects=True, vmem_limit_bytes=56 * 2**20
        ),
    )(attn, gate, up, down, gains, terms)


def total_of(own, others):
    return own.astype(jnp.float32) + jnp.sum(others.astype(jnp.float32), axis=0)


def own_block(array, kind, axis=0):
    return lax.dynamic_index_in_dim(array, group_place(kind), axis, keepdims=False)


def per_device(
    tokens,
    positions,
    norm1_gain,
    w_query,
    w_key,
    w_value,
    w_out,
    norm2_gain,
    w_gate,
    w_up,
    w_down,
    out_grad,
):
    piece = norm1_gain.shape[0]
    gains = jnp.stack([norm1_gain, norm2_gain])
    gains = jnp.pad(gains, ((0, 14), (0, -piece % 128)))
    qkv_w, gate_w, out_w, up_w, down_w, gains, grad_all = gather_weights(
        1,
        (0, 0, 1, 1, 1),
        (jnp.concatenate([w_query, w_key, w_value], axis=1), w_gate, w_out, w_up, w_down.T),
        gains,
        out_grad,
    )
    qkv_w, gate_w, out_w, up_w, down_w, grad_all = (
        array.reshape(-1, array.shape[-1])
        for array in (qkv_w, gate_w, out_w, up_w, down_w, grad_all)
    )
    gain_one = gains[:, 0, :piece].reshape(-1)
    gain_two = gains[:, 1, :piece].reshape(-1)
    shard_rows = tokens.shape[0]
    width = tokens.shape[1]
    seq_len = positions.shape[0]
    query_groups = QUERY_HEADS // KEY_VALUE_HEADS
    key_value_width = KEY_VALUE_HEADS * HEAD_SIZE
    head_scale = 1.0 / math.sqrt(HEAD_SIZE)
    gain_one = gain_one.astype(jnp.float32)
    gain_two = gain_two.astype(jnp.float32)
    group_rank = lax.axis_index("ctx") * lax.axis_size("tp") + lax.axis_index("tp")
    own_place = lax.dynamic_slice_in_dim(positions, group_rank * shard_rows, shard_rows)
    residual = tokens.astype(jnp.float32)
    normed_one, inverse_one = norm_rows(residual)
    first_hidden = (normed_one * gain_one).astype(jnp.bfloat16)
    projected = jnp.dot(first_hidden, qkv_w, preferred_element_type=jnp.float32)
    unrotated_query = projected[:, :width]
    unrotated_key = projected[:, width : width + key_value_width]
    value_rows = projected[:, width + key_value_width :].astype(jnp.bfloat16)
    cosine_table, sine_table = rope_tables(own_place, HEAD_SIZE)
    query_tensor = apply_rotary(
        unrotated_query.reshape(shard_rows, QUERY_HEADS, HEAD_SIZE), cosine_table, sine_table
    ).astype(jnp.bfloat16)
    query_tensor = query_tensor.reshape(shard_rows, KEY_VALUE_HEADS, query_groups, HEAD_SIZE)
    key_row_list = apply_rotary(
        unrotated_key.reshape(shard_rows, KEY_VALUE_HEADS, HEAD_SIZE), cosine_table, sine_table
    ).astype(jnp.bfloat16)
    key_row_list = key_row_list.reshape(shard_rows, key_value_width)
    (gathered,) = spread(2, jnp.concatenate([key_row_list, value_rows], axis=1))
    gathered = gathered.reshape(seq_len, 2 * key_value_width)
    gathered_keys = gathered[:, :key_value_width]
    gathered_values = gathered[:, key_value_width:]
    block_size = 512
    pair_count = seq_len // block_size
    blocked_keys = gathered_keys.reshape(pair_count, block_size, KEY_VALUE_HEADS, HEAD_SIZE)
    blocked_values = gathered_values.reshape(pair_count, block_size, KEY_VALUE_HEADS, HEAD_SIZE)
    place_blocks = positions.reshape(pair_count, block_size)

    def forward_block(carry, items):
        run_max, run_total, run_acc = carry
        key_block, value_block, key_place = items
        allowed = key_place[None, :] <= own_place[:, None]
        scores = (
            jnp.einsum(
                "qhgd,khd->hgqk", query_tensor, key_block, preferred_element_type=jnp.float32
            )
            * head_scale
        )
        scores = jnp.where(allowed, scores, negative_large)
        new_max = jnp.maximum(run_max, jnp.max(scores, axis=-1))
        weights = jnp.where(allowed, jnp.exp(scores - new_max[..., None]), 0.0)
        factor = jnp.exp(run_max - new_max)
        run_total = run_total * factor + jnp.sum(weights, axis=-1)
        run_acc = run_acc * factor[..., None] + jnp.einsum(
            "hgqk,khd->hgqd",
            weights.astype(jnp.bfloat16),
            value_block,
            preferred_element_type=jnp.float32,
        )
        return ((new_max, run_total, run_acc), None)

    start_carry = (
        jnp.full((KEY_VALUE_HEADS, query_groups, shard_rows), negative_large, jnp.float32),
        jnp.zeros((KEY_VALUE_HEADS, query_groups, shard_rows), jnp.float32),
        jnp.zeros((KEY_VALUE_HEADS, query_groups, shard_rows, HEAD_SIZE), jnp.float32),
    )
    (run_max, run_total, run_acc), _ = lax.scan(
        forward_block, start_carry, (blocked_keys, blocked_values, place_blocks)
    )
    log_total = run_max + jnp.log(run_total)
    attention_output = jnp.transpose(run_acc / run_total[..., None], (2, 0, 1, 3))
    attention_low = attention_output.reshape(shard_rows, width).astype(jnp.bfloat16)
    middle = residual + jnp.dot(attention_low, out_w, preferred_element_type=jnp.float32)
    normed_two, inverse_two = norm_rows(middle)
    hidden_two = (normed_two * gain_two).astype(jnp.bfloat16)
    (mlp_input,) = exchange(3, (hidden_two, "tp", "gather"))
    mlp_input = mlp_input.reshape(-1, width)
    gate = jnp.dot(mlp_input, gate_w, preferred_element_type=jnp.float32)
    upper = jnp.dot(mlp_input, up_w, preferred_element_type=jnp.float32)
    sigma = jax.nn.sigmoid(gate)
    active = gate * sigma
    inner = (active * upper).astype(jnp.bfloat16)
    mlp_output = jnp.einsum("rf,df->rd", inner, down_w, preferred_element_type=jnp.float32)
    mlp_output = mlp_output.astype(jnp.bfloat16).reshape(-1, shard_rows, width)
    grad_inner = jnp.einsum("rd,df->rf", grad_all, down_w, preferred_element_type=jnp.float32)
    grad_down_w = jnp.einsum("rf,rd->df", inner, grad_all, preferred_element_type=jnp.float32)
    grad_gate = (grad_inner * upper * sigma * (1.0 + gate * (1.0 - sigma))).astype(jnp.bfloat16)
    grad_upper = (grad_inner * active).astype(jnp.bfloat16)
    grad_gate_w = jnp.einsum("rd,rf->df", mlp_input, grad_gate, preferred_element_type=jnp.float32)
    grad_up_w = jnp.einsum("rd,rf->df", mlp_input, grad_upper, preferred_element_type=jnp.float32)
    grad_hidden_two = (
        jnp.einsum("rf,df->rd", grad_gate, gate_w, preferred_element_type=jnp.float32)
        + jnp.einsum("rf,df->rd", grad_upper, up_w, preferred_element_type=jnp.float32)
    ).astype(jnp.bfloat16)
    grad_hidden_two = grad_hidden_two.reshape(-1, shard_rows, width)
    (hidden_terms,) = exchange(4, (grad_hidden_two, "tp", "first"))
    grad_hidden_two = total_of(own_block(grad_hidden_two, "tp"), hidden_terms)
    grad_middle_norm, grad_gain_two = norm_back(grad_hidden_two, normed_two, inverse_two, gain_two)
    grad_middle = out_grad.astype(jnp.float32) + grad_middle_norm
    grad_middle_low = grad_middle.astype(jnp.bfloat16)
    grad_out_w = jnp.einsum(
        "rc,rd->cd", attention_low, grad_middle_low, preferred_element_type=jnp.float32
    )
    attention_gradient = jnp.einsum(
        "rd,cd->rc", grad_middle_low, out_w, preferred_element_type=jnp.float32
    )
    attention_gradient = attention_gradient.astype(jnp.bfloat16).reshape(
        shard_rows, KEY_VALUE_HEADS, query_groups, HEAD_SIZE
    )
    delta = jnp.einsum("qhgd,qhgd->hgq", attention_gradient.astype(jnp.float32), attention_output)

    def score_grads(key_block, value_block, key_place):
        allowed = key_place[None, :] <= own_place[:, None]
        scores = (
            jnp.einsum(
                "qhgd,khd->hgqk", query_tensor, key_block, preferred_element_type=jnp.float32
            )
            * head_scale
        )
        scores = jnp.where(allowed, scores, negative_large)
        weights = jnp.where(allowed, jnp.exp(scores - log_total[..., None]), 0.0)
        grad_weights = jnp.einsum(
            "qhgd,khd->hgqk", attention_gradient, value_block, preferred_element_type=jnp.float32
        )
        grad_scores = (weights * (grad_weights - delta[..., None])).astype(jnp.bfloat16)
        return (weights.astype(jnp.bfloat16), grad_scores)

    def key_value_terms(weights_low, grad_scores):
        grad_key = (
            jnp.einsum(
                "hgqk,qhgd->khd", grad_scores, query_tensor, preferred_element_type=jnp.float32
            )
            * head_scale
        )
        grad_value = jnp.einsum(
            "hgqk,qhgd->khd", weights_low, attention_gradient, preferred_element_type=jnp.float32
        )
        return (grad_key, grad_value)

    def query_term(grad_scores, key_block):
        return (
            jnp.einsum("hgqk,khd->qhgd", grad_scores, key_block, preferred_element_type=jnp.float32)
            * head_scale
        )

    query_offset = jnp.zeros((shard_rows, KEY_VALUE_HEADS, query_groups, HEAD_SIZE), jnp.float32)

    def backward_block(grad_query, items):
        key_block, value_block, key_place = items
        weights_low, grad_scores = score_grads(key_block, value_block, key_place)
        grad_key, grad_value = key_value_terms(weights_low, grad_scores)
        return (grad_query + query_term(grad_scores, key_block), (grad_key, grad_value))

    grad_query, (key_terms, value_terms) = lax.scan(
        backward_block, query_offset, (blocked_keys, blocked_values, place_blocks)
    )
    pair_terms = jnp.concatenate(
        [
            key_terms.reshape(-1, shard_rows, key_value_width),
            value_terms.reshape(-1, shard_rows, key_value_width),
        ],
        axis=-1,
    ).astype(jnp.bfloat16)
    (other_terms,) = exchange(5, (pair_terms, "all", "first"))
    pair_grads = total_of(own_block(pair_terms, "all"), other_terms)
    local_key_gradient = pair_grads[:, :key_value_width]
    grad_value_own = pair_grads[:, key_value_width:]
    grad_query_raw = (
        apply_rotary(
            grad_query.reshape(shard_rows, QUERY_HEADS, HEAD_SIZE), cosine_table, -sine_table
        )
        .astype(jnp.bfloat16)
        .reshape(shard_rows, width)
    )
    grad_key_raw = (
        apply_rotary(
            local_key_gradient.reshape(shard_rows, KEY_VALUE_HEADS, HEAD_SIZE),
            cosine_table,
            -sine_table,
        )
        .astype(jnp.bfloat16)
        .reshape(shard_rows, key_value_width)
    )
    grad_value_low = grad_value_own.astype(jnp.bfloat16)
    grad_projected = jnp.concatenate([grad_query_raw, grad_key_raw, grad_value_low], axis=1)
    grad_qkv_w = jnp.einsum(
        "rd,rc->dc", first_hidden, grad_projected, preferred_element_type=jnp.float32
    )
    grad_hidden_one = jnp.einsum(
        "rc,dc->rd", grad_projected, qkv_w, preferred_element_type=jnp.float32
    )
    grad_residual_norm, grad_gain_one = norm_back(
        grad_hidden_one, normed_one, inverse_one, gain_one
    )
    tokens_grad = (grad_middle + grad_residual_norm).astype(jnp.bfloat16)
    size_shard = group_size("shard")
    gain_grads = jnp.stack([grad_gain_one, grad_gain_two]).reshape(2, size_shard, piece)
    gain_grads = jnp.pad(gain_grads.transpose(1, 0, 2), ((0, 0), (0, 6), (0, -piece % 128)))
    grad_attention_w = jnp.concatenate(
        [grad_qkv_w.astype(jnp.bfloat16), grad_out_w.astype(jnp.bfloat16)], axis=1
    )
    attention_total, feed_total, gain_all, output_terms = reduce_weights(
        6,
        *[
            array.astype(jnp.bfloat16).reshape(size_shard, piece, array.shape[-1])
            for array in (grad_attention_w, grad_gate_w, grad_up_w, grad_down_w)
        ],
        gain_grads,
        mlp_output,
    )
    result = (middle + total_of(own_block(mlp_output, "tp"), output_terms)).astype(jnp.bfloat16)
    attention_total = attention_total.transpose(0, 2, 1, 3).reshape(-1, grad_attention_w.shape[1])
    attention_total = attention_total[:piece].astype(jnp.float32)
    feed_total = feed_total.reshape(-1, feed_total.shape[-1])[:piece].astype(jnp.float32)
    projected_width = width + 2 * key_value_width
    hidden_part = gate_w.shape[-1]
    out_query = attention_total[:, :width]
    out_key = attention_total[:, width : width + key_value_width]
    out_value = attention_total[:, width + key_value_width : projected_width]
    out_proj = attention_total[:, projected_width:]
    out_gate = feed_total[:, :hidden_part]
    out_up = feed_total[:, hidden_part : 2 * hidden_part]
    out_down = feed_total[:, 2 * hidden_part :].T
    gain_total = jnp.sum(gain_all, axis=0)
    out_gain_one = gain_total[0, :piece]
    out_gain_two = gain_total[1, :piece]
    return (
        result,
        tokens_grad,
        out_gain_one,
        out_query,
        out_key,
        out_value,
        out_proj,
        out_gain_two,
        out_gate,
        out_up,
        out_down,
    )


def solution(mesh):
    in_specs = (
        P(("shard", "ctx", "tp"), None),
        P("shard"),
        P("shard"),
        P("shard", None),
        P("shard", None),
        P("shard", None),
        P("shard", None),
        P("shard"),
        P("shard", "tp"),
        P("shard", "tp"),
        P("tp", "shard"),
        P(("shard", "ctx", "tp"), None),
    )
    out_specs = (
        P(("shard", "ctx", "tp"), None),
        P(("shard", "ctx", "tp"), None),
        P("shard"),
        P("shard", None),
        P("shard", None),
        P("shard", None),
        P("shard", None),
        P("shard"),
        P("shard", "tp"),
        P("shard", "tp"),
        P("tp", "shard"),
    )
    return jax.shard_map(
        per_device, mesh=mesh, in_specs=in_specs, out_specs=out_specs, check_vma=False
    )
```

```python
import functools
import math

import jax
import jax.numpy as jnp
from jax import lax
from jax.experimental import pallas as pl
from jax.experimental.pallas import tpu as pltpu
from jax.sharding import PartitionSpec as P

QUERY_HEADS = 15
KEY_VALUE_HEADS = 5
HEAD_SIZE = 64


norm_eps = 1e-05
rope_base = 100000.0
negative_large = -1e30


def rope_tables(block_places, head_width):
    half_width = head_width // 2
    frequency = rope_base ** (-(jnp.arange(half_width, dtype=jnp.float32) * 2.0 / head_width))
    angles = block_places.astype(jnp.float32)[:, None] * frequency[None, :]
    return (jnp.cos(angles), jnp.sin(angles))


def apply_rotary(heads, cosine_table, sine_table):
    half_width = heads.shape[-1] // 2
    first = heads[..., :half_width]
    second = heads[..., half_width:]
    cosine_rows = cosine_table[:, None, :]
    sine_rows = sine_table[:, None, :]
    return jnp.concatenate(
        [first * cosine_rows - second * sine_rows, second * cosine_rows + first * sine_rows],
        axis=-1,
    )


def norm_rows(rows):
    inverse = lax.rsqrt(jnp.mean(rows * rows, axis=-1, keepdims=True) + norm_eps)
    return (rows * inverse, inverse)


def norm_back(grad_normed, normed, inverse, gain):
    scaled = grad_normed * gain
    grad_rows = inverse * (scaled - normed * jnp.mean(scaled * normed, axis=-1, keepdims=True))
    return (grad_rows, jnp.sum(grad_normed * normed, axis=0))


MESH = pl.DeviceIdType.MESH
HBM = pl.BlockSpec(memory_space=pl.ANY)


def group_size(kind):
    shard, ctx, tp = lax.axis_size("shard"), lax.axis_size("ctx"), lax.axis_size("tp")
    return {"core": 2, "x": shard // 2, "shard": shard, "ctx": ctx, "tp": tp, "all": ctx * tp}[kind]


def group_place(kind):
    shard, ctx, tp = lax.axis_index("shard"), lax.axis_index("ctx"), lax.axis_index("tp")
    if kind == "core":
        return lax.rem(shard, 2)
    if kind == "x":
        return lax.div(shard, 2)
    if kind == "all":
        return ctx * lax.axis_size("tp") + tp
    return {"shard": shard, "ctx": ctx, "tp": tp}[kind]


def member(kind, step):
    size = group_size(kind)
    place = lax.rem(group_place(kind) + step, size)
    if kind == "core":
        return place, {"shard": 2 * lax.div(lax.axis_index("shard"), 2) + place}
    if kind == "x":
        return place, {"shard": 2 * place + lax.rem(lax.axis_index("shard"), 2)}
    if kind == "all":
        tp = lax.axis_size("tp")
        return place, {"ctx": lax.div(place, tp), "tp": lax.rem(place, tp)}
    return place, {kind: place}


def greet(kinds):
    barrier = pltpu.get_barrier_semaphore()
    total = 0
    for kind in kinds:
        for step in range(1, group_size(kind)):
            _, device = member(kind, step)
            pl.semaphore_signal(barrier, inc=1, device_id=device, device_id_type=MESH)
            total += 1
    pl.semaphore_wait(barrier, total)


def send(src, dst, sems, index, device):
    copy = pltpu.make_async_remote_copy(
        src_ref=src,
        dst_ref=dst,
        send_sem=sems.at[0, index],
        recv_sem=sems.at[1, index],
        device_id=device,
        device_id_type=MESH,
    )
    copy.start()
    return copy


def exchange_body(plan, *refs):
    count = len(plan)
    ins, outs, sems, local = refs[:count], refs[count : 2 * count], refs[-2], refs[-1]
    greet(sorted({kind for kind, _ in plan}))
    copies = []
    own = []
    index = 0
    for item, (kind, mode) in enumerate(plan):
        me = group_place(kind)
        if mode == "gather":
            copy = pltpu.make_async_copy(ins[item], outs[item].at[me], local.at[item])
            copy.start()
            own.append(copy)
    for item, (kind, mode) in enumerate(plan):
        me = group_place(kind)
        for step in range(1, group_size(kind)):
            place, device = member(kind, step)
            if mode == "gather":
                source, target = ins[item], outs[item].at[me]
            elif mode == "second":
                source, target = ins[item].at[:, place], outs[item].at[step - 1]
            else:
                source, target = ins[item].at[place], outs[item].at[step - 1]
            copies.append(send(source, target, sems, index, device))
            index += 1
    for copy in own:
        copy.wait()
    for copy in copies:
        copy.wait()


def exchange(collective_id, *items):
    plan = tuple((kind, mode) for _, kind, mode in items)
    shapes = []
    total = 0
    for array, kind, mode in items:
        size = group_size(kind)
        total += size - 1
        if mode == "gather":
            shape = (size,) + array.shape
        elif mode == "second":
            shape = (size - 1,) + array.shape[:1] + array.shape[2:]
        else:
            shape = (size - 1,) + array.shape[1:]
        shapes.append(jax.ShapeDtypeStruct(shape, array.dtype))
    return pl.pallas_call(
        functools.partial(exchange_body, plan),
        out_shape=shapes,
        in_specs=[HBM] * len(items),
        out_specs=[HBM] * len(items),
        scratch_shapes=[
            pltpu.SemaphoreType.DMA((2, total)),
            pltpu.SemaphoreType.DMA((len(items),)),
        ],
        compiler_params=pltpu.CompilerParams(collective_id=collective_id, has_side_effects=True),
    )(*[array for array, _, _ in items])


def spread_body(count, *refs):
    ins, outs, sems, local = refs[:count], refs[count : 2 * count], refs[-2], refs[-1]
    greet(("ctx", "tp"))
    ctx, tp = group_place("ctx"), group_place("tp")
    size_ctx, size_tp = group_size("ctx"), group_size("tp")
    own = []
    across = []
    onward = []
    index = 0
    for item in range(count):
        copy = pltpu.make_async_copy(ins[item], outs[item].at[ctx, tp], local.at[item])
        copy.start()
        own.append(copy)
        for step in range(1, size_tp):
            _, device = member("tp", step)
            target = outs[item].at[ctx, tp]
            across.append((item, step, send(ins[item], target, sems, index, device)))
            index += 1
        for hop in range(1, size_ctx):
            _, device = member("ctx", hop)
            target = outs[item].at[ctx, tp]
            onward.append(send(ins[item], target, sems, index, device))
            index += 1
    for item, step, copy in across:
        copy.wait_recv()
        source = outs[item].at[ctx, lax.rem(tp + size_tp - step, size_tp)]
        for hop in range(1, size_ctx):
            _, device = member("ctx", hop)
            onward.append(send(source, source, sems, index, device))
            index += 1
    for _, _, copy in across:
        copy.wait_send()
    for copy in onward:
        copy.wait()
    for copy in own:
        copy.wait()


def spread(collective_id, *arrays):
    size_ctx, size_tp = group_size("ctx"), group_size("tp")
    total = len(arrays) * (size_ctx * size_tp - 1)
    return pl.pallas_call(
        functools.partial(spread_body, len(arrays)),
        out_shape=[
            jax.ShapeDtypeStruct((size_ctx, size_tp) + array.shape, array.dtype)
            for array in arrays
        ],
        in_specs=[HBM] * len(arrays),
        out_specs=[HBM] * len(arrays),
        scratch_shapes=[
            pltpu.SemaphoreType.DMA((2, total)),
            pltpu.SemaphoreType.DMA((len(arrays),)),
        ],
        compiler_params=pltpu.CompilerParams(collective_id=collective_id, has_side_effects=True),
    )(*arrays)


def pair_device():
    ctx = lax.axis_index("ctx")
    return {"ctx": 2 * lax.div(ctx, 2) + 1 - lax.rem(ctx, 2)}


def weights_body(halves, *refs):
    count = len(halves)
    ins, outs = refs[: count + 1], refs[count + 1 : 2 * count + 2]
    sems, local = refs[-2], refs[-1]
    shard, parity = group_place("shard"), lax.rem(lax.axis_index("ctx"), 2)
    size_x = group_size("x")
    sibling = member("core", 1)[1]
    partner = pair_device()
    barrier = pltpu.get_barrier_semaphore()
    peers = [sibling, partner]
    peers += [member("x", step)[1] for step in range(1, size_x)]
    peers += [member("shard", step)[1] for step in range(1, group_size("shard"))]
    for device in peers:
        pl.semaphore_signal(barrier, inc=1, device_id=device, device_id_type=MESH)
    pl.semaphore_wait(barrier, len(peers))

    def remote(src, dst, index, device):
        return pltpu.make_async_remote_copy(
            src_ref=src,
            dst_ref=dst,
            send_sem=sems.at[0, index],
            recv_sem=sems.at[1, index],
            device_id=device,
            device_id_type=MESH,
        )

    plain = []
    for item in range(count + 1):
        copy = pltpu.make_async_copy(ins[item], outs[item].at[shard], local.at[item])
        copy.start()
        plain.append(copy)
    index = 0
    across = {}
    pieces = 3 if ins[0].shape[0] % 48 == 0 else 1
    height = ins[0].shape[0] // pieces
    for item in range(count):
        for part in range(pieces):
            cut = pl.ds(part * height, height)
            for step in range(1, size_x):
                _, device = member("x", step)
                target = outs[item].at[shard, cut]
                across[item, part, step] = remote(ins[item].at[cut], target, index, device)
                index += 1
    ahead = 3 * (size_x - 1)
    for parity_now in range(2):

        @pl.when(parity == parity_now)
        def _():
            mine = [key for key in across if halves[key[0]] == parity_now]
            for key in mine[:ahead]:
                across[key].start()

    for step in range(1, group_size("shard")):
        _, device = member("shard", step)
        plain.append(send(ins[count], outs[count].at[shard], sems, index, device))
        index += 1
    for item in range(count):
        plain.append(send(ins[item], outs[item].at[shard], sems, index, sibling))
        index += 1
    handed = {}
    for item, part, step in across:
        origin = lax.rem(shard + 2 * (size_x - step), 2 * size_x)
        block = outs[item].at[origin, pl.ds(part * height, height)]
        handed[item, part, step] = (
            remote(block, block, index, partner),
            remote(block, block, index + 1, sibling),
        )
        index += 2
    lag = 2
    for parity_now in range(2):

        @pl.when(parity == parity_now)
        def _():
            mine = [key for key in handed if halves[key[0]] == parity_now]
            others = [key for key in handed if halves[key[0]] != parity_now]
            for turn in range(max(len(mine), len(others) + lag)):
                if turn < len(mine):
                    key = mine[turn]
                    across[key].wait_recv()
                    handed[key][0].start()
                    handed[key][1].start()
                    across[key].wait_send()
                    if turn + ahead < len(mine):
                        across[mine[turn + ahead]].start()
                if lag <= turn < len(others) + lag:
                    key = others[turn - lag]
                    handed[key][0].wait_recv()
                    handed[key][1].start()
            for key in mine:
                handed[key][0].wait_send()

    for key in handed:
        handed[key][1].wait()
    for copy in plain:
        copy.wait()


def gather_weights(collective_id, halves, weights, gains):
    shard = group_size("shard")
    count = len(weights)
    pieces = 3 if weights[0].shape[0] % 48 == 0 else 1
    total = count * pieces * (shard // 2 - 1) * 3 + count + shard - 1
    return pl.pallas_call(
        functools.partial(weights_body, halves),
        out_shape=[
            jax.ShapeDtypeStruct((shard,) + array.shape, array.dtype)
            for array in (*weights, gains)
        ],
        in_specs=[HBM] * (count + 1),
        out_specs=[HBM] * (count + 1),
        scratch_shapes=[
            pltpu.SemaphoreType.DMA((2, total)),
            pltpu.SemaphoreType.DMA((count + 1,)),
        ],
        compiler_params=pltpu.CompilerParams(collective_id=collective_id, has_side_effects=True),
    )(*weights, gains)


def reduce_body(sizes, *refs):
    attn, gate, up, down, gains, terms, attn_out, feed_out, gain_out, terms_in = refs[:10]
    from_core, feed_core, attn_x, attn_x_in, attn_sum, attn_ctx_in, attn_part = refs[10:17]
    attn_tp_in, feed_sum, feed_ctx_in, feed_mid, feed_x_in, gain_in, gain_sum, sems = refs[17:]
    piece, padded = sizes
    size_x, size_ctx, size_tp = group_size("x"), group_size("ctx"), group_size("tp")
    size_shard, size_all = group_size("shard"), group_size("all")
    rows, columns = padded // size_ctx, attn.shape[-1] // size_tp
    feeds = (gate, up, down)
    hidden = gate.shape[-1]
    x, core, ctx, tp = (group_place(kind) for kind in ("x", "core", "ctx", "tp"))
    shard, all_place = group_place("shard"), group_place("all")
    greet(("shard", "all"))
    used = []

    def start(src, dst, device):
        copy = send(src, dst, sems, len(used), device)
        used.append(copy)
        return copy

    def arrived(copies):
        for copy in copies:
            copy.wait_recv()

    def add(target, *terms):
        total = terms[0].astype(jnp.float32)
        for term in terms[1:]:
            total = total + term.astype(jnp.float32)
        return total.astype(target.dtype)

    other, sibling = member("core", 1)
    attn_core = [
        start(attn.at[2 * block + other], from_core.at[block], sibling) for block in range(size_x)
    ]
    feed_core_copies = [
        start(
            feeds[item].at[2 * block + other],
            feed_core.at[item, block],
            sibling,
        )
        for item in range(3)
        for block in range(size_x)
    ]
    gain_copies = []
    for step in range(1, size_shard):
        place, device = member("shard", step)
        gain_copies.append(start(gains.at[place], gain_in.at[step - 1], device))
    term_copies = []
    for step in range(1, size_tp):
        place, device = member("tp", step)
        term_copies.append(start(terms.at[place], terms_in.at[step - 1], device))

    if padded > piece:
        attn_x[:, piece:, :] = jnp.zeros((size_x, padded - piece, attn.shape[-1]), attn.dtype)
        feed_sum[:, piece:, :] = jnp.zeros((size_x, padded - piece, 3 * hidden), attn.dtype)
    arrived(attn_core)
    for block in range(size_x):
        for at in range(0, attn.shape[-1], 640):
            cut = slice(at, at + 640)
            attn_x[block, :piece, cut] = add(
                attn_x, attn[2 * block + core, :, cut], from_core[block, :, cut]
            )
    attn_x_copies = []
    for step in range(1, size_x):
        place, device = member("x", step)
        attn_x_copies.append(start(attn_x.at[place], attn_x_in.at[step - 1], device))

    arrived(feed_core_copies)
    for item in range(3):
        for block in range(size_x):
            cut = slice(item * hidden, (item + 1) * hidden)
            feed_sum[block, :piece, cut] = add(
                feed_sum, feeds[item][2 * block + core], feed_core[item, block]
            )
    feed_ctx_copies = []
    for step in range(1, size_ctx):
        place, device = member("ctx", step)
        first = pl.multiple_of(place * rows, rows)
        feed_ctx_copies.append(
            start(feed_sum.at[:, pl.ds(first, rows)], feed_ctx_in.at[step - 1], device)
        )
    my_rows = pl.ds(pl.multiple_of(ctx * rows, rows), rows)

    arrived(gain_copies)
    gain_sum[...] = gains[shard] + jnp.sum(gain_in[...], axis=0)
    gain_out[all_place] = gain_sum[...]
    gain_last = []
    for step in range(1, size_all):
        _, device = member("all", step)
        gain_last.append(start(gain_sum, gain_out.at[all_place], device))

    arrived(feed_ctx_copies)
    for at in range(0, 3 * hidden, 640):
        cut = slice(at, at + 640)
        for block in range(size_x):
            feed_mid[block, :, cut] = add(
                feed_mid,
                feed_sum[block, my_rows, cut],
                *[feed_ctx_in[step, block, :, cut] for step in range(size_ctx - 1)],
            )
    feed_x_copies = []
    for step in range(1, size_x):
        place, device = member("x", step)
        feed_x_copies.append(start(feed_mid.at[place], feed_x_in.at[step - 1], device))

    arrived(attn_x_copies)
    for at in range(0, attn.shape[-1], 640):
        cut = slice(at, at + 640)
        attn_sum[:, cut] = add(
            attn_sum, attn_x[x, :, cut], *[attn_x_in[step, :, cut] for step in range(size_x - 1)]
        )
    attn_ctx_copies = []
    for step in range(1, size_ctx):
        place, device = member("ctx", step)
        first = pl.multiple_of(place * rows, rows)
        attn_ctx_copies.append(
            start(attn_sum.at[pl.ds(first, rows)], attn_ctx_in.at[step - 1], device)
        )

    arrived(attn_ctx_copies)
    for part in range(size_tp):
        cut = slice(part * columns, (part + 1) * columns)
        attn_part[part] = add(
            attn_part,
            attn_sum[my_rows, cut],
            *[attn_ctx_in[step, :, cut] for step in range(size_ctx - 1)],
        )
    attn_tp_copies = []
    for step in range(1, size_tp):
        place, device = member("tp", step)
        attn_tp_copies.append(start(attn_part.at[place], attn_tp_in.at[step - 1], device))

    arrived(feed_x_copies)
    for at in range(0, 3 * hidden, 640):
        cut = slice(at, at + 640)
        feed_out[ctx, :, cut] = add(
            feed_out, feed_mid[x, :, cut], *[feed_x_in[step, :, cut] for step in range(size_x - 1)]
        )
    feed_last = []
    for step in range(1, size_ctx):
        _, device = member("ctx", step)
        feed_last.append(start(feed_out.at[ctx], feed_out.at[ctx], device))

    arrived(attn_tp_copies)
    attn_out[ctx, tp] = add(
        attn_out, attn_part[tp], *[attn_tp_in[step] for step in range(size_tp - 1)]
    )
    mine = attn_out.at[ctx, tp]
    across = []
    last = []
    for step in range(1, size_tp):
        _, device = member("tp", step)
        across.append((step, start(mine, mine, device)))
    for hop in range(1, size_ctx):
        _, device = member("ctx", hop)
        last.append(start(mine, mine, device))
    for step, copy in across:
        copy.wait_recv()
        block = attn_out.at[ctx, lax.rem(tp + size_tp - step, size_tp)]
        for hop in range(1, size_ctx):
            _, device = member("ctx", hop)
            last.append(start(block, block, device))
    arrived(last)
    arrived(feed_last)
    arrived(gain_last)
    arrived(term_copies)
    for copy in used:
        copy.wait_send()


def reduce_weights(collective_id, attn, gate, up, down, gains, terms):
    size_shard, size_x, size_ctx = group_size("shard"), group_size("x"), group_size("ctx")
    size_tp, size_all = group_size("tp"), group_size("all")
    piece, width, hidden = attn.shape[1], attn.shape[2], gate.shape[2]
    unit = 16 * size_ctx
    padded = -(-piece // unit) * unit
    rows, columns = padded // size_ctx, width // size_tp
    low = attn.dtype
    total = 4 * size_x + size_shard - 1 + 2 * (size_x - 1) + 3 * (size_ctx - 1)
    total += 2 * (size_all - 1) + 2 * (size_tp - 1)
    vmem = pl.BlockSpec(memory_space=pltpu.VMEM)
    return pl.pallas_call(
        functools.partial(reduce_body, (piece, padded)),
        out_shape=[
            jax.ShapeDtypeStruct((size_ctx, size_tp, rows, columns), low),
            jax.ShapeDtypeStruct((size_ctx, rows, 3 * hidden), low),
            jax.ShapeDtypeStruct((size_all,) + gains.shape[1:], gains.dtype),
            jax.ShapeDtypeStruct((size_tp - 1,) + terms.shape[1:], terms.dtype),
        ],
        in_specs=[vmem] * 5 + [HBM],
        out_specs=[vmem] * 3 + [HBM],
        scratch_shapes=[
            pltpu.VMEM((size_x, piece, width), low),
            pltpu.VMEM((3, size_x, piece, hidden), low),
            pltpu.VMEM((size_x, padded, width), low),
            pltpu.VMEM((size_x - 1, padded, width), low),
            pltpu.VMEM((padded, width), low),
            pltpu.VMEM((size_ctx - 1, rows, width), low),
            pltpu.VMEM((size_tp, rows, columns), low),
            pltpu.VMEM((size_tp - 1, rows, columns), low),
            pltpu.VMEM((size_x, padded, 3 * hidden), low),
            pltpu.VMEM((size_ctx - 1, size_x, rows, 3 * hidden), low),
            pltpu.VMEM((size_x, rows, 3 * hidden), low),
            pltpu.VMEM((size_x - 1, rows, 3 * hidden), low),
            pltpu.VMEM((size_shard - 1,) + gains.shape[1:], gains.dtype),
            pltpu.VMEM(gains.shape[1:], gains.dtype),
            pltpu.SemaphoreType.DMA((2, total)),
        ],
        compiler_params=pltpu.CompilerParams(
            collective_id=collective_id, has_side_effects=True, vmem_limit_bytes=56 * 2**20
        ),
    )(attn, gate, up, down, gains, terms)


def total_of(own, others):
    return own.astype(jnp.float32) + jnp.sum(others.astype(jnp.float32), axis=0)


def own_block(array, kind, axis=0):
    return lax.dynamic_index_in_dim(array, group_place(kind), axis, keepdims=False)


def per_device(
    tokens,
    positions,
    norm1_gain,
    w_query,
    w_key,
    w_value,
    w_out,
    norm2_gain,
    w_gate,
    w_up,
    w_down,
    out_grad,
):
    piece = norm1_gain.shape[0]
    gains = jnp.stack([norm1_gain, norm2_gain])
    gains = jnp.pad(gains, ((0, 14), (0, -piece % 128)))
    qkv_w, gate_w, out_w, up_w, down_w, gains = gather_weights(
        1,
        (0, 0, 1, 1, 1),
        (jnp.concatenate([w_query, w_key, w_value], axis=1), w_gate, w_out, w_up, w_down.T),
        gains,
    )
    grad_all = lax.all_gather(out_grad, "tp", axis=0, tiled=True)
    qkv_w, gate_w, out_w, up_w, down_w = (
        array.reshape(-1, array.shape[-1]) for array in (qkv_w, gate_w, out_w, up_w, down_w)
    )
    gain_one = gains[:, 0, :piece].reshape(-1)
    gain_two = gains[:, 1, :piece].reshape(-1)
    shard_rows = tokens.shape[0]
    width = tokens.shape[1]
    seq_len = positions.shape[0]
    query_groups = QUERY_HEADS // KEY_VALUE_HEADS
    key_value_width = KEY_VALUE_HEADS * HEAD_SIZE
    head_scale = 1.0 / math.sqrt(HEAD_SIZE)
    gain_one = gain_one.astype(jnp.float32)
    gain_two = gain_two.astype(jnp.float32)
    group_rank = lax.axis_index("ctx") * lax.axis_size("tp") + lax.axis_index("tp")
    own_place = lax.dynamic_slice_in_dim(positions, group_rank * shard_rows, shard_rows)
    residual = tokens.astype(jnp.float32)
    normed_one, inverse_one = norm_rows(residual)
    first_hidden = (normed_one * gain_one).astype(jnp.bfloat16)
    projected = jnp.dot(first_hidden, qkv_w, preferred_element_type=jnp.float32)
    unrotated_query = projected[:, :width]
    unrotated_key = projected[:, width : width + key_value_width]
    value_rows = projected[:, width + key_value_width :].astype(jnp.bfloat16)
    cosine_table, sine_table = rope_tables(own_place, HEAD_SIZE)
    query_tensor = apply_rotary(
        unrotated_query.reshape(shard_rows, QUERY_HEADS, HEAD_SIZE), cosine_table, sine_table
    ).astype(jnp.bfloat16)
    query_tensor = query_tensor.reshape(shard_rows, KEY_VALUE_HEADS, query_groups, HEAD_SIZE)
    key_row_list = apply_rotary(
        unrotated_key.reshape(shard_rows, KEY_VALUE_HEADS, HEAD_SIZE), cosine_table, sine_table
    ).astype(jnp.bfloat16)
    key_row_list = key_row_list.reshape(shard_rows, key_value_width)
    (gathered,) = spread(2, jnp.concatenate([key_row_list, value_rows], axis=1))
    gathered = gathered.reshape(seq_len, 2 * key_value_width)
    gathered_keys = gathered[:, :key_value_width]
    gathered_values = gathered[:, key_value_width:]
    block_size = 1024
    pair_count = seq_len // block_size
    blocked_keys = gathered_keys.reshape(pair_count, block_size, KEY_VALUE_HEADS, HEAD_SIZE)
    blocked_values = gathered_values.reshape(pair_count, block_size, KEY_VALUE_HEADS, HEAD_SIZE)
    place_blocks = positions.reshape(pair_count, block_size)

    def forward_block(carry, items):
        run_max, run_total, run_acc = carry
        key_block, value_block, key_place = items
        allowed = key_place[None, :] <= own_place[:, None]
        scores = (
            jnp.einsum(
                "qhgd,khd->hgqk", query_tensor, key_block, preferred_element_type=jnp.float32
            )
            * head_scale
        )
        scores = jnp.where(allowed, scores, negative_large)
        new_max = jnp.maximum(run_max, jnp.max(scores, axis=-1))
        weights = jnp.where(allowed, jnp.exp(scores - new_max[..., None]), 0.0)
        factor = jnp.exp(run_max - new_max)
        run_total = run_total * factor + jnp.sum(weights, axis=-1)
        run_acc = run_acc * factor[..., None] + jnp.einsum(
            "hgqk,khd->hgqd",
            weights.astype(jnp.bfloat16),
            value_block,
            preferred_element_type=jnp.float32,
        )
        return ((new_max, run_total, run_acc), None)

    start_carry = (
        jnp.full((KEY_VALUE_HEADS, query_groups, shard_rows), negative_large, jnp.float32),
        jnp.zeros((KEY_VALUE_HEADS, query_groups, shard_rows), jnp.float32),
        jnp.zeros((KEY_VALUE_HEADS, query_groups, shard_rows, HEAD_SIZE), jnp.float32),
    )
    (run_max, run_total, run_acc), _ = lax.scan(
        forward_block, start_carry, (blocked_keys, blocked_values, place_blocks)
    )
    log_total = run_max + jnp.log(run_total)
    attention_output = jnp.transpose(run_acc / run_total[..., None], (2, 0, 1, 3))
    attention_low = attention_output.reshape(shard_rows, width).astype(jnp.bfloat16)
    middle = residual + jnp.dot(attention_low, out_w, preferred_element_type=jnp.float32)
    normed_two, inverse_two = norm_rows(middle)
    hidden_two = (normed_two * gain_two).astype(jnp.bfloat16)
    (mlp_input,) = exchange(3, (hidden_two, "tp", "gather"))
    mlp_input = mlp_input.reshape(-1, width)
    gate = jnp.dot(mlp_input, gate_w, preferred_element_type=jnp.float32)
    upper = jnp.dot(mlp_input, up_w, preferred_element_type=jnp.float32)
    sigma = jax.nn.sigmoid(gate)
    active = gate * sigma
    inner = (active * upper).astype(jnp.bfloat16)
    mlp_output = jnp.einsum("rf,df->rd", inner, down_w, preferred_element_type=jnp.float32)
    mlp_output = mlp_output.astype(jnp.bfloat16).reshape(-1, shard_rows, width)
    grad_inner = jnp.einsum("rd,df->rf", grad_all, down_w, preferred_element_type=jnp.float32)
    grad_down_w = jnp.einsum("rf,rd->df", inner, grad_all, preferred_element_type=jnp.float32)
    grad_gate = (grad_inner * upper * sigma * (1.0 + gate * (1.0 - sigma))).astype(jnp.bfloat16)
    grad_upper = (grad_inner * active).astype(jnp.bfloat16)
    grad_gate_w = jnp.einsum("rd,rf->df", mlp_input, grad_gate, preferred_element_type=jnp.float32)
    grad_up_w = jnp.einsum("rd,rf->df", mlp_input, grad_upper, preferred_element_type=jnp.float32)
    grad_hidden_two = (
        jnp.einsum("rf,df->rd", grad_gate, gate_w, preferred_element_type=jnp.float32)
        + jnp.einsum("rf,df->rd", grad_upper, up_w, preferred_element_type=jnp.float32)
    ).astype(jnp.bfloat16)
    grad_hidden_two = grad_hidden_two.reshape(-1, shard_rows, width)
    (hidden_terms,) = exchange(4, (grad_hidden_two, "tp", "first"))
    grad_hidden_two = total_of(own_block(grad_hidden_two, "tp"), hidden_terms)
    grad_middle_norm, grad_gain_two = norm_back(grad_hidden_two, normed_two, inverse_two, gain_two)
    grad_middle = out_grad.astype(jnp.float32) + grad_middle_norm
    grad_middle_low = grad_middle.astype(jnp.bfloat16)
    grad_out_w = jnp.einsum(
        "rc,rd->cd", attention_low, grad_middle_low, preferred_element_type=jnp.float32
    )
    attention_gradient = jnp.einsum(
        "rd,cd->rc", grad_middle_low, out_w, preferred_element_type=jnp.float32
    )
    attention_gradient = attention_gradient.astype(jnp.bfloat16).reshape(
        shard_rows, KEY_VALUE_HEADS, query_groups, HEAD_SIZE
    )
    delta = jnp.einsum("qhgd,qhgd->hgq", attention_gradient.astype(jnp.float32), attention_output)

    def score_grads(key_block, value_block, key_place):
        allowed = key_place[None, :] <= own_place[:, None]
        scores = (
            jnp.einsum(
                "qhgd,khd->hgqk", query_tensor, key_block, preferred_element_type=jnp.float32
            )
            * head_scale
        )
        scores = jnp.where(allowed, scores, negative_large)
        weights = jnp.where(allowed, jnp.exp(scores - log_total[..., None]), 0.0)
        grad_weights = jnp.einsum(
            "qhgd,khd->hgqk", attention_gradient, value_block, preferred_element_type=jnp.float32
        )
        grad_scores = (weights * (grad_weights - delta[..., None])).astype(jnp.bfloat16)
        return (weights.astype(jnp.bfloat16), grad_scores)

    def key_value_terms(weights_low, grad_scores):
        grad_key = (
            jnp.einsum(
                "hgqk,qhgd->khd", grad_scores, query_tensor, preferred_element_type=jnp.float32
            )
            * head_scale
        )
        grad_value = jnp.einsum(
            "hgqk,qhgd->khd", weights_low, attention_gradient, preferred_element_type=jnp.float32
        )
        return (grad_key, grad_value)

    def query_term(grad_scores, key_block):
        return (
            jnp.einsum("hgqk,khd->qhgd", grad_scores, key_block, preferred_element_type=jnp.float32)
            * head_scale
        )

    query_offset = jnp.zeros((shard_rows, KEY_VALUE_HEADS, query_groups, HEAD_SIZE), jnp.float32)

    def backward_block(grad_query, items):
        key_block, value_block, key_place = items
        weights_low, grad_scores = score_grads(key_block, value_block, key_place)
        grad_key, grad_value = key_value_terms(weights_low, grad_scores)
        return (grad_query + query_term(grad_scores, key_block), (grad_key, grad_value))

    grad_query, (key_terms, value_terms) = lax.scan(
        backward_block, query_offset, (blocked_keys, blocked_values, place_blocks)
    )
    pair_terms = jnp.concatenate(
        [
            key_terms.reshape(-1, shard_rows, key_value_width),
            value_terms.reshape(-1, shard_rows, key_value_width),
        ],
        axis=-1,
    ).astype(jnp.bfloat16)
    (other_terms,) = exchange(5, (pair_terms, "all", "first"))
    pair_grads = total_of(own_block(pair_terms, "all"), other_terms)
    local_key_gradient = pair_grads[:, :key_value_width]
    grad_value_own = pair_grads[:, key_value_width:]
    grad_query_raw = (
        apply_rotary(
            grad_query.reshape(shard_rows, QUERY_HEADS, HEAD_SIZE), cosine_table, -sine_table
        )
        .astype(jnp.bfloat16)
        .reshape(shard_rows, width)
    )
    grad_key_raw = (
        apply_rotary(
            local_key_gradient.reshape(shard_rows, KEY_VALUE_HEADS, HEAD_SIZE),
            cosine_table,
            -sine_table,
        )
        .astype(jnp.bfloat16)
        .reshape(shard_rows, key_value_width)
    )
    grad_value_low = grad_value_own.astype(jnp.bfloat16)
    grad_projected = jnp.concatenate([grad_query_raw, grad_key_raw, grad_value_low], axis=1)
    grad_qkv_w = jnp.einsum(
        "rd,rc->dc", first_hidden, grad_projected, preferred_element_type=jnp.float32
    )
    grad_hidden_one = jnp.einsum(
        "rc,dc->rd", grad_projected, qkv_w, preferred_element_type=jnp.float32
    )
    grad_residual_norm, grad_gain_one = norm_back(
        grad_hidden_one, normed_one, inverse_one, gain_one
    )
    tokens_grad = (grad_middle + grad_residual_norm).astype(jnp.bfloat16)
    size_shard = group_size("shard")
    gain_grads = jnp.stack([grad_gain_one, grad_gain_two]).reshape(2, size_shard, piece)
    gain_grads = jnp.pad(gain_grads.transpose(1, 0, 2), ((0, 0), (0, 6), (0, -piece % 128)))
    grad_attention_w = jnp.concatenate(
        [grad_qkv_w.astype(jnp.bfloat16), grad_out_w.astype(jnp.bfloat16)], axis=1
    )
    attention_total, feed_total, gain_all, output_terms = reduce_weights(
        6,
        *[
            array.astype(jnp.bfloat16).reshape(size_shard, piece, array.shape[-1])
            for array in (grad_attention_w, grad_gate_w, grad_up_w, grad_down_w)
        ],
        gain_grads,
        mlp_output,
    )
    result = (middle + total_of(own_block(mlp_output, "tp"), output_terms)).astype(jnp.bfloat16)
    attention_total = attention_total.transpose(0, 2, 1, 3).reshape(-1, grad_attention_w.shape[1])
    attention_total = attention_total[:piece].astype(jnp.float32)
    feed_total = feed_total.reshape(-1, feed_total.shape[-1])[:piece].astype(jnp.float32)
    projected_width = width + 2 * key_value_width
    hidden_part = gate_w.shape[-1]
    out_query = attention_total[:, :width]
    out_key = attention_total[:, width : width + key_value_width]
    out_value = attention_total[:, width + key_value_width : projected_width]
    out_proj = attention_total[:, projected_width:]
    out_gate = feed_total[:, :hidden_part]
    out_up = feed_total[:, hidden_part : 2 * hidden_part]
    out_down = feed_total[:, 2 * hidden_part :].T
    gain_total = jnp.sum(gain_all, axis=0)
    out_gain_one = gain_total[0, :piece]
    out_gain_two = gain_total[1, :piece]
    return (
        result,
        tokens_grad,
        out_gain_one,
        out_query,
        out_key,
        out_value,
        out_proj,
        out_gain_two,
        out_gate,
        out_up,
        out_down,
    )


def solution(mesh):
    in_specs = (
        P(("shard", "ctx", "tp"), None),
        P("shard"),
        P("shard"),
        P("shard", None),
        P("shard", None),
        P("shard", None),
        P("shard", None),
        P("shard"),
        P("shard", "tp"),
        P("shard", "tp"),
        P("tp", "shard"),
        P(("shard", "ctx", "tp"), None),
    )
    out_specs = (
        P(("shard", "ctx", "tp"), None),
        P(("shard", "ctx", "tp"), None),
        P("shard"),
        P("shard", None),
        P("shard", None),
        P("shard", None),
        P("shard", None),
        P("shard"),
        P("shard", "tp"),
        P("shard", "tp"),
        P("tp", "shard"),
    )
    return jax.shard_map(
        per_device, mesh=mesh, in_specs=in_specs, out_specs=out_specs, check_vma=False
    )
```
